32 devices in a mesh: arrow: 4 (over x, core), blk: 8 (over z, y).
Axes of the slice: x: 2, y: 2, z: 4, core: 2. Of those that a mesh axis runs over, the one named last changes fastest.
Arguments:
- features: bfloat16 [8192, 512], P(('arrow', 'blk')), may hold values from -6 to 6
- positions: int32 [4, 8192], P(None, ('arrow', 'blk')), may hold values from 0 to 8191, as said below
- diag_values: bfloat16 [4096, 8192], P('arrow', 'blk'), may hold values from -0.1875 to 0.1875
- column_values: bfloat16 [4096, 8192], P('arrow', 'blk'), may hold values from -0.1875 to 0.1875
- row_values: bfloat16 [4096, 8192], P('arrow', 'blk'), may hold values from -0.0625 to 0.0625
- tile_masks: int32 [3, 32, 64], P(None, 'arrow', 'blk'), may hold values from 0 to 1, as said below
- up_weight: bfloat16 [1024, 4096], replicated, may hold values from -0.1875 to 0.1875
- down_weight: bfloat16 [4096, 512], replicated, may hold values from -0.09375 to 0.09375
Outputs:
- node_out: bfloat16 [8192, 512], P(('arrow', 'blk'))
The draws below stay inside these ranges and needn't reach their ends.
Inputs may be any that keep to these rules, and one draw needn't show every extreme that they name: For each arrow, positions is a permutation of the nodes. The 256 nodes of one device put at most 48 nodes into any one block of 1024 positions of one arrow, and exactly 48 into some block. `tile_masks`: 1 marks a stored tile, 0 an empty one.
All inputs are finite; a program needn't handle non-finite values.
Results may differ from the reference program's by a relative error of at most 0.0085.
Values may be sent and summed in bfloat16 or wider, within the bound.
A program may use at most 64 MiB of HBM per device.

```python
import jax
import jax.numpy as jnp
from jax import lax

F = 512
FF = 4096
R = 256
BS = 1024
NT = 8
NODES = 8192
N_ARROW = 4
N_BLK = 8


def draw_positions(key, part):
    block_count = NODES // BS
    arrow_count = BS // R
    device_count = arrow_count * block_count
    base_count = R // block_count
    half_spread = max(R // (2 * block_count), 1)
    source = jnp.arange(device_count, dtype=jnp.int32)
    column = jnp.arange(block_count, dtype=jnp.int32)
    rank_ids = jnp.arange(R, dtype=jnp.int32)

    def one_arrow(arrow_key):
        sub_keys = jax.random.split(arrow_key, 4)
        spread = jax.random.randint(sub_keys[0], (block_count // 2,), -half_spread, half_spread + 1, dtype=jnp.int32)
        spread = spread.at[0].set(half_spread)
        shifts = jax.random.permutation(sub_keys[1], jnp.concatenate([spread, -spread])).astype(jnp.int32)
        counts = base_count + shifts[(column[None, :] - source[:, None]) % block_count]
        upper_cum = jnp.cumsum(counts, axis=1)
        lower_cum = upper_cum - counts
        target = jnp.sum((upper_cum[:, None, :] <= rank_ids[None, :, None]).astype(jnp.int32), axis=2)
        inner_rank = rank_ids[None, :] - jnp.take_along_axis(lower_cum, target, axis=1)
        offset = jnp.cumsum(counts, axis=0) - counts
        slot_pos = jnp.take_along_axis(offset, target, axis=1) + inner_rank
        orders = jax.vmap(lambda sub_key: jax.random.permutation(sub_key, R).astype(jnp.int32))(jax.random.split(sub_keys[2], device_count))
        shuffles = jax.vmap(lambda sub_key: jax.random.permutation(sub_key, BS).astype(jnp.int32))(jax.random.split(sub_keys[3], block_count))
        final_pos = target * BS + shuffles[target, slot_pos]
        node_ids = source[:, None] * R + orders
        return jnp.zeros((NODES,), jnp.int32).at[node_ids.reshape(-1)].set(final_pos.reshape(-1))
    return jax.vmap(one_arrow)(jax.random.split(jax.random.fold_in(key, 11), arrow_count))


def draw_tile_masks(key, part):
    block_count = NODES // BS
    arrow_count = BS // R
    sub_keys = jax.random.split(jax.random.fold_in(key, 23), 2)
    density = jax.random.randint(sub_keys[0], (3, arrow_count, 1, block_count, 1), 1, 5, dtype=jnp.int32)
    coin_flips = jax.random.randint(sub_keys[1], (3, arrow_count, NT, block_count, NT), 0, 4, dtype=jnp.int32)
    return (coin_flips < density).astype(jnp.int32).reshape(3, arrow_count * NT, block_count * NT)


def levels(key, dims, cuts, smallest, top_value):
    gain, own = 1.0, jax.random.fold_in(key, 6)
    for axis_at, blocks in cuts:
        steps = jnp.exp(jax.random.uniform(jax.random.fold_in(own, axis_at), (blocks,), jnp.float32, smallest / len(cuts), top_value / len(cuts)))
        gain = gain * jnp.repeat(steps, dims[axis_at] // blocks).reshape([-1 if axis == axis_at else 1 for axis in range(len(dims))])
    return gain


def noise(own_key, shape, scale, bound, shards=(), kind=jnp.bfloat16):
    factor_of = levels(own_key, shape, shards, -0.22, 0.18) if shards else 1.0
    result = jax.random.normal(own_key, shape, jnp.float32) * scale * factor_of
    return jnp.minimum(jnp.maximum(result, -bound), bound).astype(kind)


def setup_inputs(seed: int = 0) -> dict:
    key_list = jax.random.split(jax.random.key(seed), 9)
    features = noise(key_list[0], (NODES, F), 1.0, 6.0, ((0, 32),))
    positions = draw_positions(jax.random.fold_in(key_list[8], 71), 0)
    diag_values = noise(key_list[2], (N_ARROW * BS, N_BLK * BS), BS ** -0.5, 0.1875, ((0, 4), (1, 8)))
    column_values = noise(key_list[3], (N_ARROW * BS, N_BLK * BS), BS ** -0.5, 0.1875, ((0, 4), (1, 8)))
    row_values = noise(key_list[4], (N_ARROW * BS, N_BLK * BS), NODES ** -0.5, 0.0625, ((0, 4), (1, 8)))
    tile_masks = draw_tile_masks(jax.random.fold_in(key_list[8], 71), 0)
    up_weight = noise(key_list[6], (2 * F, FF), (2 * F) ** -0.5, 0.1875)
    down_weight = noise(key_list[7], (FF, F), FF ** -0.5, 0.09375)
    return {"features": features, "positions": positions, "diag_values": diag_values, "column_values": column_values, "row_values": row_values, "tile_masks": tile_masks, "up_weight": up_weight, "down_weight": down_weight}


def masked_block(values, tiles):
    tile_count = tiles.shape[0]
    tile_edge = values.shape[0] // tile_count
    shaped = values.reshape(tile_count, tile_edge, tile_count, tile_edge)
    keep_mask = tiles.astype(values.dtype)[:, None, :, None]
    return (shaped * keep_mask).reshape(values.shape)


def reference(features, positions, diag_values, column_values, row_values, tile_masks, up_weight, down_weight):
    feat_width = features.shape[1]
    block_count = NODES // BS
    arrow_count = BS // R
    total = jnp.zeros((NODES, feat_width), jnp.float32)
    for arrow_id in range(arrow_count):
        ordered = jnp.zeros_like(features).at[positions[arrow_id]].set(features)
        block_feats = ordered.reshape(block_count, BS, feat_width)
        head_block = block_feats[0]

        def split_blocks(values):
            return values[arrow_id * BS:(arrow_id + 1) * BS].reshape(BS, block_count, BS).transpose(1, 0, 2)

        def split_masks(kind):
            return tile_masks[kind, arrow_id * NT:(arrow_id + 1) * NT].reshape(NT, block_count, NT).transpose(1, 0, 2)

        stacked = (split_blocks(diag_values), split_blocks(column_values), split_blocks(row_values),
                   split_masks(0), split_masks(1), split_masks(2), block_feats)

        def one_block(items):
            diag_part, column_part, row_part, diag_mask, column_mask, row_mask, local_feats = items
            local_sum = jnp.dot(masked_block(diag_part, diag_mask), local_feats, preferred_element_type=jnp.float32)
            local_sum = local_sum + jnp.dot(masked_block(column_part, column_mask), head_block, preferred_element_type=jnp.float32)
            arm_term = jnp.dot(masked_block(row_part, row_mask), local_feats, preferred_element_type=jnp.float32)
            return local_sum, arm_term

        local_sums, arm_terms = lax.map(one_block, stacked)
        arm_total = jnp.sum(arm_terms, axis=0)
        results = local_sums.at[0].add(arm_total).astype(jnp.bfloat16).reshape(NODES, feat_width)
        total = total + results[positions[arrow_id]].astype(jnp.float32)
    aggregate = total.astype(jnp.bfloat16)
    joined = jnp.concatenate([features, aggregate], axis=1)
    hidden = jax.nn.silu(jnp.dot(joined, up_weight, preferred_element_type=jnp.float32)).astype(jnp.bfloat16)
    return jnp.dot(hidden, down_weight, preferred_element_type=jnp.float32).astype(jnp.bfloat16)
```

```python
import functools

import jax
import jax.numpy as jnp
from jax import lax
from jax.experimental import pallas as pl
from jax.experimental.pallas import tpu as pltpu
from jax.sharding import PartitionSpec as P

MESH = pl.DeviceIdType.MESH


def gather_kernel(dims, shard_ref, x_ref, xh_ref, st_ref, held, pos, rank, packed, sth,
                  zs, zr, xs, xr, ys, yr, dxs, dxr, dys, dyr, cs, cr, own_sem):
    nb, rows, cap, block_rows = dims
    lines = nb // 2
    n_dev = 4 * nb
    padded, width = shard_ref.shape
    half = (padded // 2 + 15) // 16 * 16
    a, b = lax.axis_index("arrow"), lax.axis_index("blk")
    ao, c, bo, bi = a // 2, a % 2, b // 2, b % 2
    up, down = (a, b + 2), (a, b - 2)
    across = ((1 - ao) * 2 + c, b)
    beside = (a, bo * 2 + 1 - bi)
    core = (ao * 2 + 1 - c, b)

    def column(ao_, c_, bi_):
        return (ao_ * 2 + c_) * 2 + bi_

    mine = column(ao, c, bi)
    x_col = column(1 - ao, c, bi)
    y_col = column(ao, c, 1 - bi)
    d_col = column(1 - ao, c, 1 - bi)
    cols = (mine, x_col, y_col, d_col)
    other = (column(ao, 1 - c, bi), column(1 - ao, 1 - c, bi), column(ao, 1 - c, 1 - bi),
             column(1 - ao, 1 - c, 1 - bi))
    whole_rows = pl.ds(0, padded)
    top, low = pl.ds(0, half), pl.ds(half, padded - half)

    def send(col, k, part, ssem, rsem, device):
        view = held.at[col, k, part]
        return pltpu.make_async_remote_copy(
            src_ref=view, dst_ref=view, send_sem=ssem, recv_sem=rsem,
            device_id=device, device_id_type=MESH)

    def z_up(k):
        return send(mine, k, whole_rows, zs.at[0, k], zr.at[k], up)

    def z_down(k):
        return send(mine, k, whole_rows, zs.at[1, k], zr.at[k], down)

    def x_send(k):
        return send(mine, k, whole_rows, xs.at[k], xr.at[k], across)

    def y_send(k):
        return send(mine, k, whole_rows, ys.at[k], yr.at[k], beside)

    def dy_send(k):
        return send(x_col, k, top, dys.at[k], dyr.at[k], beside)

    def dx_send(k):
        return send(y_col, k, low, dxs.at[k], dxr.at[k], across)

    def core_send(kind, k):
        return send(cols[kind], k, whole_rows, cs.at[kind, k], cr.at[kind, k], core)

    own = pltpu.make_async_copy(shard_ref, held.at[mine, bo], own_sem)
    own.start()
    barrier = pltpu.get_barrier_semaphore()
    for device in (across, beside, core):
        pl.semaphore_signal(barrier, inc=1, device_id=device, device_id_type=MESH)

    @pl.when(bo < lines - 1)
    def _():
        pl.semaphore_signal(barrier, inc=1, device_id=up, device_id_type=MESH)

    @pl.when(bo > 0)
    def _():
        pl.semaphore_signal(barrier, inc=1, device_id=down, device_id_type=MESH)

    ends = (bo < lines - 1).astype(jnp.int32) + (bo > 0).astype(jnp.int32)
    pl.semaphore_wait(barrier, 3 + ends)

    own.wait()

    def step(t, carry):
        for sign in (-1, 1):
            k = bo + sign * t
            ok = (k >= 0) & (k < lines) & (t < lines)
            if sign == 1:
                ok = ok & (t > 0)

            @pl.when(ok)
            def _():
                @pl.when(t > 0)
                def _():
                    send(mine, k, whole_rows, zs.at[0, k], zr.at[k], up).wait_recv()

                @pl.when((k <= bo) & (bo < lines - 1))
                def _():
                    z_up(k).start()

                @pl.when((k >= bo) & (bo > 0))
                def _():
                    z_down(k).start()

                x_send(k).start()
                y_send(k).start()
                core_send(0, k).start()

        for sign in (-1, 1):
            t2 = t - 1
            k2 = bo + sign * t2
            ok2 = (k2 >= 0) & (k2 < lines) & (t2 >= 0) & (t2 < lines)
            if sign == 1:
                ok2 = ok2 & (t2 > 0)

            @pl.when(ok2)
            def _():
                send(x_col, k2, whole_rows, xs.at[k2], xr.at[k2], across).wait_recv()
                dy_send(k2).start()
                core_send(1, k2).start()
                send(y_col, k2, whole_rows, ys.at[k2], yr.at[k2], beside).wait_recv()
                dx_send(k2).start()
                core_send(2, k2).start()

        for sign in (-1, 1):
            t3 = t - 2
            k3 = bo + sign * t3
            ok3 = (k3 >= 0) & (k3 < lines) & (t3 >= 0)
            if sign == 1:
                ok3 = ok3 & (t3 > 0)

            @pl.when(ok3)
            def _():
                send(d_col, k3, top, dys.at[k3], dyr.at[k3], beside).wait_recv()
                send(d_col, k3, low, dxs.at[k3], dxr.at[k3], across).wait_recv()
                core_send(3, k3).start()

        return carry

    lax.fori_loop(0, lines + 2, step, 0)

    def arrive(k, carry):
        for kind in range(4):
            send(other[kind], k, whole_rows, cs.at[kind, k], cr.at[kind, k], core).wait_recv()
        return carry

    lax.fori_loop(0, lines, arrive, 0)

    extra = padded - rows
    row_id = lax.broadcasted_iota(jnp.int32, (extra, rows), 0)
    weight = jnp.where(row_id == 2 * a, 256.0, jnp.where(row_id == 2 * a + 1, 1.0, 0.0))

    def read_pos(s, carry):
        sa, sb = s // nb, s % nb
        digits = held[sa * 2 + sb % 2, sb // 2, pl.ds(rows, extra), pl.ds(0, rows)]
        pos[pl.ds(s, 1), :] = jnp.sum(digits.astype(jnp.float32) * weight, axis=0, keepdims=True)
        return carry

    lax.fori_loop(0, n_dev, read_pos, 0)
    every = pos[...].astype(jnp.int32)
    before = (lax.broadcasted_iota(jnp.int32, (rows, rows), 0)
              < lax.broadcasted_iota(jnp.int32, (rows, rows), 1)).astype(jnp.float32).astype(jnp.bfloat16)
    for kind, block in ((0, b), (1, 0)):
        inside = (every >= block * block_rows) & (every < (block + 1) * block_rows)
        count = jnp.dot(inside.astype(jnp.float32).astype(jnp.bfloat16), before,
                        preferred_element_type=jnp.float32)
        rank[kind] = jnp.where(inside, count, -1.0)

    slot_id = lax.broadcasted_iota(jnp.int32, (cap, rows), 0).astype(jnp.float32)
    lane_id = lax.broadcasted_iota(jnp.int32, (cap, block_rows), 1).astype(jnp.float32)

    def pack(s, carry):
        sa, sb = s // nb, s % nb
        place = pos[pl.ds(s, 1), :]
        source = held[sa * 2 + sb % 2, sb // 2, pl.ds(0, rows), :]
        at = pl.multiple_of(s * cap, 16)
        for kind, block, out in ((0, b, st_ref), (1, 0, sth)):
            match = slot_id == rank[kind, pl.ds(s, 1), :]
            base = (block * block_rows).astype(jnp.float32) if kind == 0 else 0.0
            where = jnp.sum(jnp.where(match, place - base + 1.0, 0.0), axis=1, keepdims=True) - 1.0
            out[pl.ds(at, cap), :] = jnp.where(lane_id == where, 1.0, 0.0).astype(jnp.bfloat16)
            chosen = jnp.where(match, 1.0, 0.0).astype(jnp.bfloat16)
            packed[kind, pl.ds(at, cap), :] = jnp.dot(
                chosen, source, preferred_element_type=jnp.float32).astype(jnp.bfloat16)
        return carry

    lax.fori_loop(0, n_dev, pack, 0)
    piece = 256

    def unpack(i, carry):
        lanes = pl.ds(pl.multiple_of(i * piece, piece), piece)
        for kind, select, out in ((0, st_ref, x_ref), (1, sth, xh_ref)):
            out[lanes, :] = lax.dot_general(
                select[:, lanes], packed[kind], (((0,), (0,)), ((), ())),
                preferred_element_type=jnp.float32).astype(jnp.bfloat16)
        return carry

    lax.fori_loop(0, block_rows // piece, unpack, 0)

    def drain(k, carry):
        @pl.when((k <= bo) & (bo < lines - 1))
        def _():
            z_up(k).wait_send()

        @pl.when((k >= bo) & (bo > 0))
        def _():
            z_down(k).wait_send()

        x_send(k).wait_send()
        y_send(k).wait_send()
        dy_send(k).wait_send()
        dx_send(k).wait_send()
        for kind in range(4):
            core_send(kind, k).wait_send()
        return carry

    lax.fori_loop(0, lines, drain, 0)


def gather_blocks(features, positions, nb, cap, block_rows):
    rows, width = features.shape
    n_dev = 4 * nb
    lines = nb // 2
    digits = jnp.stack([positions // 256, positions % 256], axis=1).reshape(-1, rows)
    digits = jnp.pad(digits, ((0, 16 - digits.shape[0]), (0, width - rows))).astype(features.dtype)
    shard = jnp.concatenate([features, digits], axis=0)
    padded = rows + 16
    slots = n_dev * cap
    dma = pltpu.SemaphoreType.DMA
    vmem = pl.BlockSpec(memory_space=pltpu.VMEM)
    bf16 = jnp.bfloat16
    return pl.pallas_call(
        functools.partial(gather_kernel, (nb, rows, cap, block_rows)),
        out_shape=(
            jax.ShapeDtypeStruct((block_rows, width), bf16),
            jax.ShapeDtypeStruct((block_rows, width), bf16),
            jax.ShapeDtypeStruct((slots, block_rows), bf16),
        ),
        in_specs=[vmem],
        out_specs=(vmem, vmem, vmem),
        scratch_shapes=[
            pltpu.VMEM((8, lines, padded, width), bf16),
            pltpu.VMEM((n_dev, rows), jnp.float32),
            pltpu.VMEM((2, n_dev, rows), jnp.float32),
            pltpu.VMEM((2, slots, width), bf16),
            pltpu.VMEM((slots, block_rows), bf16),
            dma((2, lines)), dma((lines,)),
            dma((lines,)), dma((lines,)), dma((lines,)), dma((lines,)),
            dma((lines,)), dma((lines,)), dma((lines,)), dma((lines,)),
            dma((4, lines)), dma((4, lines)), dma(()),
        ],
        compiler_params=pltpu.CompilerParams(
            collective_id=0, has_side_effects=True, vmem_limit_bytes=60 * 2**20),
        name="gather_blocks",
    )(shard)


def masked_block(values, tiles):
    tile_count = tiles.shape[0]
    tile_edge = values.shape[0] // tile_count
    shaped = values.reshape(tile_count, tile_edge, tile_count, tile_edge)
    keep_mask = tiles.astype(values.dtype)[:, None, :, None]
    return (shaped * keep_mask).reshape(values.shape)


def body(
    features, positions, diag_values, column_values, row_values, tile_masks, up_weight, down_weight
):
    rows, width = features.shape
    arrow_count = positions.shape[0]
    nb = lax.axis_size("blk")
    n_dev = arrow_count * nb
    block_rows = diag_values.shape[0]
    capacity = rows // nb + max(rows // (2 * nb), 1)
    cap = (capacity + 15) // 16 * 16
    x, x_head, select = gather_blocks(features, positions, nb, cap, block_rows)
    dot = functools.partial(jnp.dot, preferred_element_type=jnp.float32)
    arm_term = dot(masked_block(row_values, tile_masks[2]), x).astype(jnp.bfloat16)
    local_sum = dot(masked_block(diag_values, tile_masks[0]), x)
    local_sum = local_sum + dot(masked_block(column_values, tile_masks[1]), x_head)
    is_head = lax.axis_index("blk") == 0
    arm_total = lax.psum(arm_term, "blk").astype(jnp.float32)
    results = jnp.where(is_head, local_sum + arm_total, local_sum).astype(jnp.bfloat16)
    picked = dot(select, results).astype(jnp.bfloat16)
    returned = lax.all_to_all(
        picked.reshape(n_dev, cap, width), ("arrow", "blk"), split_axis=0, concat_axis=0, tiled=True
    ).reshape(n_dev * cap, width)
    inside = (positions // block_rows)[:, None, :] == jnp.arange(nb, dtype=jnp.int32)[None, :, None]
    inside = inside.reshape(n_dev, rows)
    before = (jnp.arange(rows)[:, None] < jnp.arange(rows)[None, :]).astype(jnp.bfloat16)
    rank = jnp.where(inside, dot(inside.astype(jnp.bfloat16), before), -1.0).astype(jnp.int32)
    pick = (rank.T[:, :, None] == jnp.arange(cap, dtype=jnp.int32)[None, None, :]).astype(jnp.bfloat16)
    aggregate = dot(pick.reshape(rows, n_dev * cap), returned).astype(jnp.bfloat16)
    joined = jnp.concatenate([features, aggregate], axis=1)
    hidden = jax.nn.silu(dot(joined, up_weight)).astype(jnp.bfloat16)
    return dot(hidden, down_weight).astype(jnp.bfloat16)


def solution(mesh):
    in_specs = (
        P(("arrow", "blk"), None),
        P(None, ("arrow", "blk")),
        P("arrow", "blk"),
        P("arrow", "blk"),
        P("arrow", "blk"),
        P(None, "arrow", "blk"),
        P(),
        P(),
    )
    out_specs = P(("arrow", "blk"), None)
    return jax.shard_map(body, mesh=mesh, in_specs=in_specs, out_specs=out_specs, check_vma=False)
```

```python
import functools

import jax
import jax.numpy as jnp
from jax import lax
from jax.experimental import pallas as pl
from jax.experimental.pallas import tpu as pltpu
from jax.sharding import PartitionSpec as P

MESH = pl.DeviceIdType.MESH


def gather_kernel(dims, shard_ref, x_ref, xh_ref, st_ref, sth, held, pos, rank, packed, zs, zr, xs, xr, ys, yr, dxs, dxr, dys, dyr, cs, cr, own_sem):
    nb, rows, cap, block_rows = dims
    lines = nb // 2
    n_dev = 4 * nb
    padded, width = shard_ref.shape
    half = (padded // 2 + 15) // 16 * 16
    a, b = lax.axis_index("arrow"), lax.axis_index("blk")
    ao, c, bo, bi = a // 2, a % 2, b // 2, b % 2
    up, down = (a, b + 2), (a, b - 2)
    across = ((1 - ao) * 2 + c, b)
    beside = (a, bo * 2 + 1 - bi)
    core = (ao * 2 + 1 - c, b)

    def column(ao_, c_, bi_):
        return (ao_ * 2 + c_) * 2 + bi_

    mine = column(ao, c, bi)
    x_col = column(1 - ao, c, bi)
    y_col = column(ao, c, 1 - bi)
    d_col = column(1 - ao, c, 1 - bi)
    cols = (mine, x_col, y_col, d_col)
    other = (column(ao, 1 - c, bi), column(1 - ao, 1 - c, bi), column(ao, 1 - c, 1 - bi),
             column(1 - ao, 1 - c, 1 - bi))
    whole_rows = pl.ds(0, padded)
    top, low = pl.ds(0, half), pl.ds(half, padded - half)

    def send(col, k, part, ssem, rsem, device):
        view = held.at[col, k, part]
        return pltpu.make_async_remote_copy(
            src_ref=view, dst_ref=view, send_sem=ssem, recv_sem=rsem,
            device_id=device, device_id_type=MESH)

    def z_up(k):
        return send(mine, k, whole_rows, zs.at[0, k], zr.at[k], up)

    def z_down(k):
        return send(mine, k, whole_rows, zs.at[1, k], zr.at[k], down)

    def x_send(k):
        return send(mine, k, whole_rows, xs.at[k], xr.at[k], across)

    def y_send(k):
        return send(mine, k, whole_rows, ys.at[k], yr.at[k], beside)

    def dy_send(k):
        return send(x_col, k, top, dys.at[k], dyr.at[k], beside)

    def dx_send(k):
        return send(y_col, k, low, dxs.at[k], dxr.at[k], across)

    def core_send(kind, k):
        return send(cols[kind], k, whole_rows, cs.at[kind, k], cr.at[kind, k], core)

    own = pltpu.make_async_copy(shard_ref, held.at[mine, bo], own_sem)
    own.start()
    barrier = pltpu.get_barrier_semaphore()
    for device in (across, beside, core):
        pl.semaphore_signal(barrier, inc=1, device_id=device, device_id_type=MESH)

    @pl.when(bo < lines - 1)
    def _():
        pl.semaphore_signal(barrier, inc=1, device_id=up, device_id_type=MESH)

    @pl.when(bo > 0)
    def _():
        pl.semaphore_signal(barrier, inc=1, device_id=down, device_id_type=MESH)

    ends = (bo < lines - 1).astype(jnp.int32) + (bo > 0).astype(jnp.int32)
    pl.semaphore_wait(barrier, 3 + ends)

    own.wait()

    def step(t, carry):
        for sign in (-1, 1):
            k = bo + sign * t
            ok = (k >= 0) & (k < lines) & (t < lines)
            if sign == 1:
                ok = ok & (t > 0)

            @pl.when(ok)
            def _():
                @pl.when(t > 0)
                def _():
                    send(mine, k, whole_rows, zs.at[0, k], zr.at[k], up).wait_recv()

                @pl.when((k <= bo) & (bo < lines - 1))
                def _():
                    z_up(k).start()

                @pl.when((k >= bo) & (bo > 0))
                def _():
                    z_down(k).start()

                x_send(k).start()
                y_send(k).start()
                core_send(0, k).start()

        for sign in (-1, 1):
            t2 = t - 1
            k2 = bo + sign * t2
            ok2 = (k2 >= 0) & (k2 < lines) & (t2 >= 0) & (t2 < lines)
            if sign == 1:
                ok2 = ok2 & (t2 > 0)

            @pl.when(ok2)
            def _():
                send(x_col, k2, whole_rows, xs.at[k2], xr.at[k2], across).wait_recv()
                dy_send(k2).start()
                core_send(1, k2).start()
                send(y_col, k2, whole_rows, ys.at[k2], yr.at[k2], beside).wait_recv()
                dx_send(k2).start()
                core_send(2, k2).start()

        for sign in (-1, 1):
            t3 = t - 2
            k3 = bo + sign * t3
            ok3 = (k3 >= 0) & (k3 < lines) & (t3 >= 0)
            if sign == 1:
                ok3 = ok3 & (t3 > 0)

            @pl.when(ok3)
            def _():
                send(d_col, k3, top, dys.at[k3], dyr.at[k3], beside).wait_recv()
                send(d_col, k3, low, dxs.at[k3], dxr.at[k3], across).wait_recv()
                core_send(3, k3).start()

        return carry

    lax.fori_loop(0, lines + 2, step, 0)

    def arrive(k, carry):
        for kind in range(4):
            send(other[kind], k, whole_rows, cs.at[kind, k], cr.at[kind, k], core).wait_recv()
        return carry

    lax.fori_loop(0, lines, arrive, 0)

    extra = padded - rows
    row_id = lax.broadcasted_iota(jnp.int32, (extra, rows), 0)
    weight = jnp.where(row_id == 2 * a, 256.0, jnp.where(row_id == 2 * a + 1, 1.0, 0.0))

    def read_pos(s, carry):
        sa, sb = s // nb, s % nb
        digits = held[sa * 2 + sb % 2, sb // 2, pl.ds(rows, extra), pl.ds(0, rows)]
        pos[pl.ds(s, 1), :] = jnp.sum(digits.astype(jnp.float32) * weight, axis=0, keepdims=True)
        return carry

    lax.fori_loop(0, n_dev, read_pos, 0)
    every = pos[...].astype(jnp.int32)
    before = (lax.broadcasted_iota(jnp.int32, (rows, rows), 0)
              < lax.broadcasted_iota(jnp.int32, (rows, rows), 1)).astype(jnp.float32).astype(jnp.bfloat16)
    for kind, block in ((0, b), (1, 0)):
        inside = (every >= block * block_rows) & (every < (block + 1) * block_rows)
        count = jnp.dot(inside.astype(jnp.float32).astype(jnp.bfloat16), before,
                        preferred_element_type=jnp.float32)
        rank[kind] = jnp.where(inside, count, -1.0)

    slot_id = lax.broadcasted_iota(jnp.int32, (cap, rows), 0).astype(jnp.float32)
    lane_id = lax.broadcasted_iota(jnp.int32, (cap, block_rows), 1).astype(jnp.float32)

    def pack(s, carry):
        sa, sb = s // nb, s % nb
        place = pos[pl.ds(s, 1), :]
        source = held[sa * 2 + sb % 2, sb // 2, pl.ds(0, rows), :]
        at = pl.multiple_of((sb * 4 + sa) * cap, 16)
        for kind, block, out in ((0, b, st_ref), (1, 0, sth)):
            match = slot_id == rank[kind, pl.ds(s, 1), :]
            base = (block * block_rows).astype(jnp.float32) if kind == 0 else 0.0
            where = jnp.sum(jnp.where(match, place - base + 1.0, 0.0), axis=1, keepdims=True) - 1.0
            out[pl.ds(at, cap), :] = jnp.where(lane_id == where, 1.0, 0.0).astype(jnp.bfloat16)
            chosen = jnp.where(match, 1.0, 0.0).astype(jnp.bfloat16)
            packed[kind, pl.ds(at, cap), :] = jnp.dot(
                chosen, source, preferred_element_type=jnp.float32).astype(jnp.bfloat16)
        return carry

    lax.fori_loop(0, n_dev, pack, 0)
    piece = 256

    def unpack(i, carry):
        lanes = pl.ds(pl.multiple_of(i * piece, piece), piece)
        for kind, select, out in ((0, st_ref, x_ref), (1, sth, xh_ref)):
            out[lanes, :] = lax.dot_general(
                select[:, lanes], packed[kind], (((0,), (0,)), ((), ())),
                preferred_element_type=jnp.float32).astype(jnp.bfloat16)
        return carry

    lax.fori_loop(0, block_rows // piece, unpack, 0)

    def drain(k, carry):
        @pl.when((k <= bo) & (bo < lines - 1))
        def _():
            z_up(k).wait_send()

        @pl.when((k >= bo) & (bo > 0))
        def _():
            z_down(k).wait_send()

        x_send(k).wait_send()
        y_send(k).wait_send()
        dy_send(k).wait_send()
        dx_send(k).wait_send()
        for kind in range(4):
            core_send(kind, k).wait_send()
        return carry

    lax.fori_loop(0, lines, drain, 0)


def gather_blocks(features, positions, nb, cap, block_rows):
    rows, width = features.shape
    n_dev = 4 * nb
    lines = nb // 2
    digits = jnp.stack([positions // 256, positions % 256], axis=1).reshape(-1, rows)
    digits = jnp.pad(digits, ((0, 16 - digits.shape[0]), (0, width - rows))).astype(features.dtype)
    shard = jnp.concatenate([features, digits], axis=0)
    padded = rows + 16
    slots = n_dev * cap
    dma = pltpu.SemaphoreType.DMA
    vmem = pl.BlockSpec(memory_space=pltpu.VMEM)
    bf16 = jnp.bfloat16
    return pl.pallas_call(
        functools.partial(gather_kernel, (nb, rows, cap, block_rows)),
        out_shape=(
            jax.ShapeDtypeStruct((block_rows, width), bf16),
            jax.ShapeDtypeStruct((block_rows, width), bf16),
            jax.ShapeDtypeStruct((slots, block_rows), bf16),
            jax.ShapeDtypeStruct((slots, block_rows), bf16),
        ),
        in_specs=[vmem],
        out_specs=(vmem, vmem, vmem, vmem),
        scratch_shapes=[
            pltpu.VMEM((8, lines, padded, width), bf16),
            pltpu.VMEM((n_dev, rows), jnp.float32),
            pltpu.VMEM((2, n_dev, rows), jnp.float32),
            pltpu.VMEM((2, slots, width), bf16),
            dma((2, lines)), dma((lines,)),
            dma((lines,)), dma((lines,)), dma((lines,)), dma((lines,)),
            dma((lines,)), dma((lines,)), dma((lines,)), dma((lines,)),
            dma((4, lines)), dma((4, lines)), dma(()),
        ],
        compiler_params=pltpu.CompilerParams(
            collective_id=0, has_side_effects=True, vmem_limit_bytes=60 * 2**20),
        name="gather_blocks",
    )(shard)


def return_kernel(dims, x_ref, xh_ref, st_ref, sth_ref, pick_ref, arm_pick_ref, mask_ref, diag_hbm,
                  column_hbm, row_hbm, agg_ref, blocks, arm, results, slots_arm, beside_in, up_in,
                  down_in, summed, total, arm_back, picked, returned, load_sem, ysend, yrecv, usend,
                  urecv, dsend, drecv, asend, arecv, rsend, rrecv):
    nb, cap = dims
    lines = nb // 2
    n_dev = 4 * nb
    group = 4 * cap
    block_rows, width = x_ref.shape
    a, b = lax.axis_index("arrow"), lax.axis_index("blk")
    bo, bi = b // 2, b % 2
    me = b * 4 + a
    beside, up, down = (a, bo * 2 + 1 - bi), (a, b + 2), (a, b - 2)
    f32, bf16 = jnp.float32, jnp.bfloat16
    tile = block_rows // mask_ref.shape[1]

    loads = [pltpu.make_async_copy(ref, blocks.at[i], load_sem.at[i])
             for i, ref in enumerate((row_hbm, diag_hbm, column_hbm))]
    for load in loads:
        load.start()

    barrier = pltpu.get_barrier_semaphore()

    def greet(s, carry):
        @pl.when(s != me)
        def _():
            pl.semaphore_signal(barrier, inc=1, device_id=(s % 4, s // 4), device_id_type=MESH)
        return carry

    lax.fori_loop(0, n_dev, greet, 0)
    pl.semaphore_wait(barrier, n_dev - 1)

    def remote(src, dst, ssem, rsem, device):
        return pltpu.make_async_remote_copy(src_ref=src, dst_ref=dst, send_sem=ssem, recv_sem=rsem,
                                            device_id=device, device_id_type=MESH)

    def y_copy(k):
        return remote(slots_arm.at[k * 2 + 1 - bi], beside_in.at[k], ysend.at[k], yrecv.at[k], beside)

    def up_copy(k):
        return remote(summed.at[k], up_in.at[k], usend.at[k], urecv.at[k], up)

    def down_copy(k):
        return remote(summed.at[k], down_in.at[k], dsend.at[k], drecv.at[k], down)

    def arm_copy(to, frm):
        return remote(total.at[pl.ds(pl.multiple_of(to * cap, 16), cap)],
                      arm_back.at[pl.ds(pl.multiple_of(frm * cap, 16), cap)],
                      asend.at[to], arecv.at[frm], (to, b))

    def back_copy(to, frm):
        return remote(picked.at[to], returned.at[pl.ds(pl.multiple_of(frm * cap, 16), cap)],
                      rsend.at[to], rrecv.at[frm], (to % 4, to // 4))

    def masked(kind, i):
        rows = pl.ds(pl.multiple_of(i * tile, tile), tile)
        return blocks[kind, rows, :] * mask_ref[kind, pl.ds(i, 1), :].astype(bf16)

    loads[0].wait()

    def arm_tile(i, carry):
        rows = pl.ds(pl.multiple_of(i * tile, tile), tile)
        arm[rows, :] = jnp.dot(masked(0, i), x_ref[...], preferred_element_type=f32).astype(bf16)
        return carry

    lax.fori_loop(0, block_rows // tile, arm_tile, 0)

    def place_arm(k):
        rows = pl.ds(pl.multiple_of(k * group, 16), group)
        slots_arm[k] = jnp.dot(sth_ref[rows, :], arm[...], preferred_element_type=f32).astype(bf16)

    def far_first(d, body):
        for sign in (-1, 1):
            k = bo + sign * d
            ok = (k >= 0) & (k < lines)
            if sign == 1:
                ok = ok & (d > 0)
            pl.when(ok)(functools.partial(body, k))

    def to_beside(i, carry):
        def one(k):
            place_arm(k * 2 + 1 - bi)
            y_copy(k).start()
        far_first(lines - 1 - i, one)
        return carry

    lax.fori_loop(0, lines, to_beside, 0)

    def own_arm(k, carry):
        place_arm(k * 2 + bi)
        return carry

    lax.fori_loop(0, lines, own_arm, 0)
    loads[1].wait()
    loads[2].wait()

    def block_tile(i, carry):
        rows = pl.ds(pl.multiple_of(i * tile, tile), tile)
        results[rows, :] = (
            jnp.dot(masked(1, i), x_ref[...], preferred_element_type=f32)
            + jnp.dot(masked(2, i), xh_ref[...], preferred_element_type=f32)).astype(bf16)
        return carry

    lax.fori_loop(0, block_rows // tile, block_tile, 0)

    def send_plane(k):
        plane = 2 * group
        rows = pl.ds(pl.multiple_of(k * plane, 16), plane)
        found = jnp.dot(st_ref[rows, :], results[...], preferred_element_type=f32).astype(bf16)
        picked[pl.ds(k * 8, 8)] = found.reshape(8, cap, width)

        def one(i, carry):
            to = k * 8 + i

            @pl.when(to != me)
            def _():
                back_copy(to, me).start()
            return carry

        lax.fori_loop(0, 8, one, 0)

    send_plane(bo)
    returned[pl.ds(pl.multiple_of(me * cap, 16), cap), :] = picked[me]

    def pair_sum(k):
        y_copy(k).wait_recv()
        return slots_arm[k * 2 + bi].astype(f32) + beside_in[k].astype(f32)

    def outward(i, carry):
        d = lines - 1 - i

        def one(k):
            summed[k] = pair_sum(k).astype(bf16)

            @pl.when((k > bo) & (bo > 0))
            def _():
                up_copy(k).wait_recv()
                summed[k] = (summed[k].astype(f32) + up_in[k].astype(f32)).astype(bf16)

            @pl.when((k < bo) & (bo < lines - 1))
            def _():
                down_copy(k).wait_recv()
                summed[k] = (summed[k].astype(f32) + down_in[k].astype(f32)).astype(bf16)

            @pl.when(k > bo)
            def _():
                up_copy(k).start()

            @pl.when(k < bo)
            def _():
                down_copy(k).start()

            send_plane(k)

        far_first(d, one)
        return carry

    lax.fori_loop(0, lines - 1, outward, 0)
    total[...] = pair_sum(bo).astype(bf16)

    @pl.when(bo > 0)
    def _():
        up_copy(bo).wait_recv()
        total[...] = (total[...].astype(f32) + up_in[bo].astype(f32)).astype(bf16)

    @pl.when(bo < lines - 1)
    def _():
        down_copy(bo).wait_recv()
        total[...] = (total[...].astype(f32) + down_in[bo].astype(f32)).astype(bf16)

    for to in range(4):
        @pl.when(to != a)
        def _():
            arm_copy(to, a).start()

    tail = arm_back.shape[0] - group
    arm_back[pl.ds(group, tail), :] = jnp.zeros((tail, width), bf16)
    own = pl.ds(pl.multiple_of(a * cap, 16), cap)
    arm_back[own, :] = total[own, :]

    def collect(s, carry):
        @pl.when(s != me)
        def _():
            back_copy(me, s).wait_recv()
            back_copy(s, me).wait_send()
        return carry

    lax.fori_loop(0, n_dev, collect, 0)
    for frm in range(4):
        @pl.when(frm != a)
        def _():
            arm_copy(a, frm).wait_recv()
            arm_copy(frm, a).wait_send()

    agg_ref[...] = (
        jnp.dot(pick_ref[...], returned[...], preferred_element_type=f32)
        + jnp.dot(arm_pick_ref[...], arm_back[...], preferred_element_type=f32)).astype(bf16)

    def drain(k, carry):
        y_copy(k).wait_send()

        @pl.when(k > bo)
        def _():
            up_copy(k).wait_send()

        @pl.when(k < bo)
        def _():
            down_copy(k).wait_send()
        return carry

    lax.fori_loop(0, lines, drain, 0)


def return_rows(x, xh, select, select_head, pick, arm_pick, masks, diag, column, row, nb, cap):
    block_rows, width = x.shape
    n_dev = 4 * nb
    lines = nb // 2
    group = 4 * cap
    dma = pltpu.SemaphoreType.DMA
    vmem = pl.BlockSpec(memory_space=pltpu.VMEM)
    hbm = pl.BlockSpec(memory_space=pl.ANY)
    bf16 = jnp.bfloat16
    return pl.pallas_call(
        functools.partial(return_kernel, (nb, cap)),
        out_shape=jax.ShapeDtypeStruct((pick.shape[0], width), bf16),
        in_specs=[vmem] * 7 + [hbm] * 3,
        out_specs=vmem,
        scratch_shapes=[
            pltpu.VMEM((3, block_rows, block_rows), bf16),
            pltpu.VMEM((block_rows, width), bf16),
            pltpu.VMEM((block_rows, width), bf16),
            pltpu.VMEM((nb, group, width), bf16),
            pltpu.VMEM((lines, group, width), bf16),
            pltpu.VMEM((lines, group, width), bf16),
            pltpu.VMEM((lines, group, width), bf16),
            pltpu.VMEM((lines, group, width), bf16),
            pltpu.VMEM((group, width), bf16),
            pltpu.VMEM((arm_pick.shape[1], width), bf16),
            pltpu.VMEM((n_dev, cap, width), bf16),
            pltpu.VMEM((n_dev * cap, width), bf16),
            dma((3,)), dma((lines,)), dma((lines,)), dma((lines,)), dma((lines,)),
            dma((lines,)), dma((lines,)), dma((4,)), dma((4,)), dma((n_dev,)), dma((n_dev,)),
        ],
        compiler_params=pltpu.CompilerParams(
            collective_id=1, has_side_effects=True, vmem_limit_bytes=56 * 2**20),
        name="return_rows",
    )(x, xh, select, select_head, pick, arm_pick, masks, diag, column, row)


def body(
    features, positions, diag_values, column_values, row_values, tile_masks, up_weight, down_weight
):
    rows, width = features.shape
    arrow_count = positions.shape[0]
    nb = lax.axis_size("blk")
    n_dev = arrow_count * nb
    block_rows = diag_values.shape[0]
    capacity = rows // nb + max(rows // (2 * nb), 1)
    cap = (capacity + 15) // 16 * 16
    dot = functools.partial(jnp.dot, preferred_element_type=jnp.float32)
    x, x_head, select, select_head = gather_blocks(features, positions, nb, cap, block_rows)
    inside = (positions // block_rows)[None] == jnp.arange(nb, dtype=jnp.int32)[:, None, None]
    inside = inside.reshape(n_dev, rows)
    before = (jnp.arange(rows)[:, None] < jnp.arange(rows)[None, :]).astype(jnp.bfloat16)
    rank = jnp.where(inside, dot(inside.astype(jnp.bfloat16), before), -1.0).astype(jnp.int32)
    pick = (rank.T[:, :, None] == jnp.arange(cap, dtype=jnp.int32)[None, None, :]).astype(jnp.bfloat16)
    pick = pick.reshape(rows, n_dev * cap)
    group = arrow_count * cap
    arm_pick = jnp.pad(pick[:, :group], ((0, 0), (0, (group // 128 + 1) * 128 - group)))
    masks = jnp.repeat(tile_masks, block_rows // tile_masks.shape[2], axis=2).astype(jnp.float32)
    masks = jnp.stack([masks[2], masks[0], masks[1]])
    aggregate = return_rows(x, x_head, select, select_head, pick, arm_pick, masks,
                            diag_values, column_values, row_values, nb, cap)
    joined = jnp.concatenate([features, aggregate], axis=1)
    hidden = jax.nn.silu(dot(joined, up_weight)).astype(jnp.bfloat16)
    return dot(hidden, down_weight).astype(jnp.bfloat16)


def solution(mesh):
    in_specs = (
        P(("arrow", "blk"), None),
        P(None, ("arrow", "blk")),
        P("arrow", "blk"),
        P("arrow", "blk"),
        P("arrow", "blk"),
        P(None, "arrow", "blk"),
        P(),
        P(),
    )
    out_specs = P(("arrow", "blk"), None)
    return jax.shard_map(body, mesh=mesh, in_specs=in_specs, out_specs=out_specs, check_vma=False)
```

```python
import functools

import jax
import jax.numpy as jnp
from jax import lax
from jax.experimental import pallas as pl
from jax.experimental.pallas import tpu as pltpu
from jax.sharding import PartitionSpec as P

MESH = pl.DeviceIdType.MESH


def gather_kernel(dims, features_ref, positions_ref, x_ref, xh_ref, st_ref, sth_ref, rank_ref, held,
                  digit_buf, packed, place_col, place_row, zs, zr, xs, xr, ys, yr, dxs, dxr, dys, dyr, cs, cr, own_sem):
    nb, rows, cap, block_rows = dims
    lines = nb // 2
    n_dev = 4 * nb
    width = features_ref.shape[1]
    padded = rows + 16
    f32, bf16 = jnp.float32, jnp.bfloat16
    half = (padded // 2 + 15) // 16 * 16
    a, b = lax.axis_index("arrow"), lax.axis_index("blk")
    ao, c, bo, bi = a // 2, a % 2, b // 2, b % 2
    up, down = (a, b + 2), (a, b - 2)
    across = ((1 - ao) * 2 + c, b)
    beside = (a, bo * 2 + 1 - bi)
    core = (ao * 2 + 1 - c, b)

    def column(ao_, c_, bi_):
        return (ao_ * 2 + c_) * 2 + bi_

    mine = column(ao, c, bi)
    x_col = column(1 - ao, c, bi)
    y_col = column(ao, c, 1 - bi)
    d_col = column(1 - ao, c, 1 - bi)
    cols = (mine, x_col, y_col, d_col)
    other = (column(ao, 1 - c, bi), column(1 - ao, 1 - c, bi), column(ao, 1 - c, 1 - bi),
             column(1 - ao, 1 - c, 1 - bi))
    whole_rows = pl.ds(0, padded)
    top, low = pl.ds(0, half), pl.ds(half, padded - half)

    def send(col, k, part, ssem, rsem, device):
        view = held.at[col, k, part]
        return pltpu.make_async_remote_copy(
            src_ref=view, dst_ref=view, send_sem=ssem, recv_sem=rsem,
            device_id=device, device_id_type=MESH)

    def z_up(k):
        return send(mine, k, whole_rows, zs.at[0, k], zr.at[k], up)

    def z_down(k):
        return send(mine, k, whole_rows, zs.at[1, k], zr.at[k], down)

    def x_send(k):
        return send(mine, k, whole_rows, xs.at[k], xr.at[k], across)

    def y_send(k):
        return send(mine, k, whole_rows, ys.at[k], yr.at[k], beside)

    def dy_send(k):
        return send(x_col, k, top, dys.at[k], dyr.at[k], beside)

    def dx_send(k):
        return send(y_col, k, low, dxs.at[k], dxr.at[k], across)

    def core_send(kind, k):
        return send(cols[kind], k, whole_rows, cs.at[kind, k], cr.at[kind, k], core)

    own = pltpu.make_async_copy(features_ref, held.at[mine, bo, pl.ds(0, rows)], own_sem)
    own.start()
    place = positions_ref[...]
    digit_buf[...] = jnp.zeros(digit_buf.shape, f32)
    digit_buf[pl.ds(0, 4), pl.ds(0, rows)] = (place // 256).astype(f32)
    digit_buf[pl.ds(4, 4), pl.ds(0, rows)] = (place % 256).astype(f32)
    held[mine, bo, pl.ds(rows, 16), :] = digit_buf[...].astype(bf16)
    barrier = pltpu.get_barrier_semaphore()
    for device in (across, beside, core):
        pl.semaphore_signal(barrier, inc=1, device_id=device, device_id_type=MESH)

    @pl.when(bo < lines - 1)
    def _():
        pl.semaphore_signal(barrier, inc=1, device_id=up, device_id_type=MESH)

    @pl.when(bo > 0)
    def _():
        pl.semaphore_signal(barrier, inc=1, device_id=down, device_id_type=MESH)

    ends = (bo < lines - 1).astype(jnp.int32) + (bo > 0).astype(jnp.int32)
    pl.semaphore_wait(barrier, 3 + ends)

    own.wait()

    q_row = lax.broadcasted_iota(jnp.int32, (16, 16), 0)
    q_lane = lax.broadcasted_iota(jnp.int32, (16, 16), 1)
    before = (lax.broadcasted_iota(jnp.int32, (rows, rows), 0)
              < lax.broadcasted_iota(jnp.int32, (rows, rows), 1)).astype(f32).astype(bf16)

    def ranks(digits, arrow, base):
        weight = jnp.where(q_lane == arrow, 256.0, jnp.where(q_lane == arrow + 4, 1.0, 0.0)).astype(bf16)
        place = jnp.dot(weight, digits, preferred_element_type=f32)
        inside = (place >= base) & (place < base + block_rows)
        count = jnp.dot(jnp.where(inside, 1.0, 0.0).astype(bf16), before, preferred_element_type=f32)
        return place - base, jnp.where(inside, count, -1.0)

    slot_id = lax.broadcasted_iota(jnp.int32, (cap, rows), 0).astype(f32)
    lane_id = lax.broadcasted_iota(jnp.int32, (cap, block_rows), 1).astype(f32)
    block_base = jnp.where(lax.broadcasted_iota(jnp.int32, (16, rows), 0) == 0,
                           (b * block_rows).astype(f32), 0.0)

    def pack(col, k):
        at = pl.multiple_of(((k * 2 + col % 2) * 4 + col // 2) * cap, 16)
        place, rank = ranks(held[col, k, pl.ds(rows, 16), pl.ds(0, rows)], a, block_base)
        chosen = []
        for kind, out in ((0, st_ref), (1, sth_ref)):
            match = slot_id == rank[kind:kind + 1, :]
            where = jnp.sum(jnp.where(match, place[kind:kind + 1, :] + 1.0, 0.0),
                            axis=1, keepdims=True) - 1.0
            out[pl.ds(at, cap), :] = jnp.where(lane_id == where, 1.0, 0.0).astype(bf16)
            place_col[kind, pl.ds(at, cap), :] = jnp.broadcast_to(where, (cap, 128))
            chosen.append(jnp.where(match, 1.0, 0.0).astype(bf16))
        found = jnp.dot(jnp.concatenate(chosen, axis=0), held[col, k, pl.ds(0, rows), :],
                        preferred_element_type=f32).astype(bf16)
        packed[0, pl.ds(at, cap), :] = found[:cap]
        packed[1, pl.ds(at, cap), :] = found[cap:]

    def step(t, carry):
        for sign in (-1, 1):
            k = bo + sign * t
            ok = (k >= 0) & (k < lines) & (t < lines)
            if sign == 1:
                ok = ok & (t > 0)

            @pl.when(ok)
            def _():
                @pl.when(t > 0)
                def _():
                    send(mine, k, whole_rows, zs.at[0, k], zr.at[k], up).wait_recv()

                @pl.when((k <= bo) & (bo < lines - 1))
                def _():
                    z_up(k).start()

                @pl.when((k >= bo) & (bo > 0))
                def _():
                    z_down(k).start()

                x_send(k).start()
                y_send(k).start()
                core_send(0, k).start()

        for sign in (-1, 1):
            t2 = t - 1
            k2 = bo + sign * t2
            ok2 = (k2 >= 0) & (k2 < lines) & (t2 >= 0) & (t2 < lines)
            if sign == 1:
                ok2 = ok2 & (t2 > 0)

            @pl.when(ok2)
            def _():
                send(x_col, k2, whole_rows, xs.at[k2], xr.at[k2], across).wait_recv()
                dy_send(k2).start()
                core_send(1, k2).start()
                send(y_col, k2, whole_rows, ys.at[k2], yr.at[k2], beside).wait_recv()
                dx_send(k2).start()
                core_send(2, k2).start()

        for sign in (-1, 1):
            t3 = t - 2
            k3 = bo + sign * t3
            ok3 = (k3 >= 0) & (k3 < lines) & (t3 >= 0)
            if sign == 1:
                ok3 = ok3 & (t3 > 0)

            @pl.when(ok3)
            def _():
                send(d_col, k3, top, dys.at[k3], dyr.at[k3], beside).wait_recv()
                send(d_col, k3, low, dxs.at[k3], dxr.at[k3], across).wait_recv()
                core_send(3, k3).start()

        def visit(i, inner):
            sign, kind, far = i % 2 * 2 - 1, i // 2 % 4, i // 8
            late = t - (kind + 1) // 2 - far
            k = bo + sign * late
            ok = (late >= 0) & (late < lines) & (k >= 0) & (k < lines) & ((late > 0) | (sign < 0))
            col = column((ao + kind % 2) % 2, (c + far) % 2, (bi + kind // 2) % 2)

            @pl.when(ok)
            def _():
                @pl.when(far == 1)
                def _():
                    send(col, k, whole_rows, cs.at[kind, k], cr.at[kind, k], core).wait_recv()

                pack(col, k)
            return inner

        lax.fori_loop(0, 16, visit, 0)
        return carry

    lax.fori_loop(0, lines + 3, step, 0)

    q = lax.broadcasted_iota(jnp.int32, (16, rows), 0)
    plane_base = jnp.where(q < 8, (bo * 2 + q % 2) * block_rows, jnp.where(q < 12, 0, -block_rows)).astype(f32)
    plane_arrow = jnp.where(q_row < 8, q_row // 2, q_row % 4)

    def plane_ranks(k, carry):
        rank_ref[k] = ranks(held[mine, k, pl.ds(rows, 16), pl.ds(0, rows)], plane_arrow, plane_base)[1]
        return carry

    lax.fori_loop(0, lines, plane_ranks, 0)

    def turn(i, carry):
        part = pl.ds(pl.multiple_of(i * 128, 128), 128)
        for kind in range(2):
            place_row[kind, :, part] = place_col[kind, part, :].T[0:8, :]
        return carry

    lax.fori_loop(0, place_row.shape[2] // 128, turn, 0)
    piece = 256
    row_id = lax.broadcasted_iota(jnp.int32, (piece, place_row.shape[2]), 0).astype(f32)

    def unpack(i, carry):
        part = pl.ds(pl.multiple_of(i * piece, piece), piece)
        for kind, out in ((0, x_ref), (1, xh_ref)):
            target = place_row[kind, 0:1, :] - (i * piece).astype(f32)
            select = jnp.where(row_id == target, 1.0, 0.0).astype(bf16)
            out[part, :] = jnp.dot(select, packed[kind], preferred_element_type=f32).astype(bf16)
        return carry

    lax.fori_loop(0, block_rows // piece, unpack, 0)

    def drain(k, carry):
        @pl.when((k <= bo) & (bo < lines - 1))
        def _():
            z_up(k).wait_send()

        @pl.when((k >= bo) & (bo > 0))
        def _():
            z_down(k).wait_send()

        x_send(k).wait_send()
        y_send(k).wait_send()
        dy_send(k).wait_send()
        dx_send(k).wait_send()
        for kind in range(4):
            core_send(kind, k).wait_send()
        return carry

    lax.fori_loop(0, lines, drain, 0)


def gather_blocks(features, positions, nb, cap, block_rows):
    rows, width = features.shape
    n_dev = 4 * nb
    lines = nb // 2
    padded = rows + 16
    slots = n_dev * cap
    dma = pltpu.SemaphoreType.DMA
    vmem = pl.BlockSpec(memory_space=pltpu.VMEM)
    bf16 = jnp.bfloat16
    return pl.pallas_call(
        functools.partial(gather_kernel, (nb, rows, cap, block_rows)),
        out_shape=(
            jax.ShapeDtypeStruct((block_rows, width), bf16),
            jax.ShapeDtypeStruct((block_rows, width), bf16),
            jax.ShapeDtypeStruct((slots, block_rows), bf16),
            jax.ShapeDtypeStruct((slots, block_rows), bf16),
            jax.ShapeDtypeStruct((lines, 16, rows), jnp.float32),
        ),
        in_specs=[vmem, vmem],
        out_specs=(vmem,) * 5,
        scratch_shapes=[
            pltpu.VMEM((8, lines, padded, width), bf16),
            pltpu.VMEM((16, width), jnp.float32),
            pltpu.VMEM((2, slots, width), bf16),
            pltpu.VMEM((2, slots, 128), jnp.float32),
            pltpu.VMEM((2, 8, slots), jnp.float32),
            dma((2, lines)), dma((lines,)),
            dma((lines,)), dma((lines,)), dma((lines,)), dma((lines,)),
            dma((lines,)), dma((lines,)), dma((lines,)), dma((lines,)),
            dma((4, lines)), dma((4, lines)), dma(()),
        ],
        compiler_params=pltpu.CompilerParams(
            collective_id=0, has_side_effects=True, vmem_limit_bytes=60 * 2**20),
        name="gather_blocks",
    )(features, positions)


def return_kernel(dims, x_ref, xh_ref, st_ref, sth_ref, pick_ref, arm_pick_ref, mask_ref, diag_hbm,
                  column_hbm, row_hbm, agg_ref, blocks, arm, results, slots_arm, beside_in, up_in,
                  down_in, summed, total, arm_back, picked, returned, load_sem, ysend, yrecv, usend,
                  urecv, dsend, drecv, asend, arecv, rsend, rrecv):
    nb, cap = dims
    lines = nb // 2
    n_dev = 4 * nb
    group = 4 * cap
    block_rows, width = x_ref.shape
    a, b = lax.axis_index("arrow"), lax.axis_index("blk")
    bo, bi = b // 2, b % 2
    me = b * 4 + a
    beside, up, down = (a, bo * 2 + 1 - bi), (a, b + 2), (a, b - 2)
    f32, bf16 = jnp.float32, jnp.bfloat16
    tile = block_rows // mask_ref.shape[1]

    loads = [pltpu.make_async_copy(ref, blocks.at[i], load_sem.at[i])
             for i, ref in enumerate((row_hbm, diag_hbm, column_hbm))]
    for load in loads:
        load.start()

    barrier = pltpu.get_barrier_semaphore()

    def greet(s, carry):
        @pl.when(s != me)
        def _():
            pl.semaphore_signal(barrier, inc=1, device_id=(s % 4, s // 4), device_id_type=MESH)
        return carry

    lax.fori_loop(0, n_dev, greet, 0)
    pl.semaphore_wait(barrier, n_dev - 1)

    def remote(src, dst, ssem, rsem, device):
        return pltpu.make_async_remote_copy(src_ref=src, dst_ref=dst, send_sem=ssem, recv_sem=rsem,
                                            device_id=device, device_id_type=MESH)

    def y_copy(k):
        return remote(slots_arm.at[k * 2 + 1 - bi], beside_in.at[k], ysend.at[k], yrecv.at[k], beside)

    def up_copy(k):
        return remote(summed.at[k], up_in.at[k], usend.at[k], urecv.at[k], up)

    def down_copy(k):
        return remote(summed.at[k], down_in.at[k], dsend.at[k], drecv.at[k], down)

    def arm_copy(to, frm):
        return remote(total.at[pl.ds(pl.multiple_of(to * cap, 16), cap)],
                      arm_back.at[pl.ds(pl.multiple_of(frm * cap, 16), cap)],
                      asend.at[to], arecv.at[frm], (to, b))

    def back_copy(to, frm):
        return remote(picked.at[to], returned.at[pl.ds(pl.multiple_of(frm * cap, 16), cap)],
                      rsend.at[to], rrecv.at[frm], (to % 4, to // 4))

    def masked(kind, i):
        rows = pl.ds(pl.multiple_of(i * tile, tile), tile)
        return blocks[kind, rows, :] * mask_ref[kind, pl.ds(i, 1), :].astype(bf16)

    loads[0].wait()

    def arm_tile(i, carry):
        rows = pl.ds(pl.multiple_of(i * tile, tile), tile)
        arm[rows, :] = jnp.dot(masked(0, i), x_ref[...], preferred_element_type=f32).astype(bf16)
        return carry

    lax.fori_loop(0, block_rows // tile, arm_tile, 0)

    def place_arm(k):
        rows = pl.ds(pl.multiple_of(k * group, 16), group)
        slots_arm[k] = jnp.dot(sth_ref[rows, :], arm[...], preferred_element_type=f32).astype(bf16)

    def far_first(d, body):
        for sign in (-1, 1):
            k = bo + sign * d
            ok = (k >= 0) & (k < lines)
            if sign == 1:
                ok = ok & (d > 0)
            pl.when(ok)(functools.partial(body, k))

    def to_beside(i, carry):
        def one(k):
            place_arm(k * 2 + 1 - bi)
            y_copy(k).start()
        far_first(lines - 1 - i, one)
        return carry

    lax.fori_loop(0, lines, to_beside, 0)

    def own_arm(k, carry):
        place_arm(k * 2 + bi)
        return carry

    lax.fori_loop(0, lines, own_arm, 0)
    loads[1].wait()
    loads[2].wait()

    def block_tile(i, carry):
        rows = pl.ds(pl.multiple_of(i * tile, tile), tile)
        results[rows, :] = (
            jnp.dot(masked(1, i), x_ref[...], preferred_element_type=f32)
            + jnp.dot(masked(2, i), xh_ref[...], preferred_element_type=f32)).astype(bf16)
        return carry

    lax.fori_loop(0, block_rows // tile, block_tile, 0)

    def send_plane(k):
        plane = 2 * group
        rows = pl.ds(pl.multiple_of(k * plane, 16), plane)
        found = jnp.dot(st_ref[rows, :], results[...], preferred_element_type=f32).astype(bf16)
        picked[pl.ds(k * 8, 8)] = found.reshape(8, cap, width)

        def one(i, carry):
            to = k * 8 + i

            @pl.when(to != me)
            def _():
                back_copy(to, me).start()
            return carry

        lax.fori_loop(0, 8, one, 0)

    send_plane(bo)
    returned[pl.ds(pl.multiple_of(me * cap, 16), cap), :] = picked[me]

    def pair_sum(k):
        y_copy(k).wait_recv()
        return slots_arm[k * 2 + bi].astype(f32) + beside_in[k].astype(f32)

    def outward(i, carry):
        d = lines - 1 - i

        def one(k):
            summed[k] = pair_sum(k).astype(bf16)

            @pl.when((k > bo) & (bo > 0))
            def _():
                up_copy(k).wait_recv()
                summed[k] = (summed[k].astype(f32) + up_in[k].astype(f32)).astype(bf16)

            @pl.when((k < bo) & (bo < lines - 1))
            def _():
                down_copy(k).wait_recv()
                summed[k] = (summed[k].astype(f32) + down_in[k].astype(f32)).astype(bf16)

            @pl.when(k > bo)
            def _():
                up_copy(k).start()

            @pl.when(k < bo)
            def _():
                down_copy(k).start()

            send_plane(k)

        far_first(d, one)
        return carry

    lax.fori_loop(0, lines - 1, outward, 0)
    total[...] = pair_sum(bo).astype(bf16)

    @pl.when(bo > 0)
    def _():
        up_copy(bo).wait_recv()
        total[...] = (total[...].astype(f32) + up_in[bo].astype(f32)).astype(bf16)

    @pl.when(bo < lines - 1)
    def _():
        down_copy(bo).wait_recv()
        total[...] = (total[...].astype(f32) + down_in[bo].astype(f32)).astype(bf16)

    for to in range(4):
        @pl.when(to != a)
        def _():
            arm_copy(to, a).start()

    tail = arm_back.shape[0] - group
    arm_back[pl.ds(group, tail), :] = jnp.zeros((tail, width), bf16)
    own = pl.ds(pl.multiple_of(a * cap, 16), cap)
    arm_back[own, :] = total[own, :]

    def collect(s, carry):
        @pl.when(s != me)
        def _():
            back_copy(me, s).wait_recv()
            back_copy(s, me).wait_send()
        return carry

    lax.fori_loop(0, n_dev, collect, 0)
    for frm in range(4):
        @pl.when(frm != a)
        def _():
            arm_copy(a, frm).wait_recv()
            arm_copy(frm, a).wait_send()

    agg_ref[...] = (
        jnp.dot(pick_ref[...], returned[...], preferred_element_type=f32)
        + jnp.dot(arm_pick_ref[...], arm_back[...], preferred_element_type=f32)).astype(bf16)

    def drain(k, carry):
        y_copy(k).wait_send()

        @pl.when(k > bo)
        def _():
            up_copy(k).wait_send()

        @pl.when(k < bo)
        def _():
            down_copy(k).wait_send()
        return carry

    lax.fori_loop(0, lines, drain, 0)


def return_rows(x, xh, select, select_head, pick, arm_pick, masks, diag, column, row, nb, cap):
    block_rows, width = x.shape
    n_dev = 4 * nb
    lines = nb // 2
    group = 4 * cap
    dma = pltpu.SemaphoreType.DMA
    vmem = pl.BlockSpec(memory_space=pltpu.VMEM)
    hbm = pl.BlockSpec(memory_space=pl.ANY)
    bf16 = jnp.bfloat16
    return pl.pallas_call(
        functools.partial(return_kernel, (nb, cap)),
        out_shape=jax.ShapeDtypeStruct((pick.shape[0], width), bf16),
        in_specs=[vmem] * 7 + [hbm] * 3,
        out_specs=vmem,
        scratch_shapes=[
            pltpu.VMEM((3, block_rows, block_rows), bf16),
            pltpu.VMEM((block_rows, width), bf16),
            pltpu.VMEM((block_rows, width), bf16),
            pltpu.VMEM((nb, group, width), bf16),
            pltpu.VMEM((lines, group, width), bf16),
            pltpu.VMEM((lines, group, width), bf16),
            pltpu.VMEM((lines, group, width), bf16),
            pltpu.VMEM((lines, group, width), bf16),
            pltpu.VMEM((group, width), bf16),
            pltpu.VMEM((arm_pick.shape[1], width), bf16),
            pltpu.VMEM((n_dev, cap, width), bf16),
            pltpu.VMEM((n_dev * cap, width), bf16),
            dma((3,)), dma((lines,)), dma((lines,)), dma((lines,)), dma((lines,)),
            dma((lines,)), dma((lines,)), dma((4,)), dma((4,)), dma((n_dev,)), dma((n_dev,)),
        ],
        compiler_params=pltpu.CompilerParams(
            collective_id=1, has_side_effects=True, vmem_limit_bytes=56 * 2**20),
        name="return_rows",
    )(x, xh, select, select_head, pick, arm_pick, masks, diag, column, row)


def body(
    features, positions, diag_values, column_values, row_values, tile_masks, up_weight, down_weight
):
    rows, width = features.shape
    arrow_count = positions.shape[0]
    nb = lax.axis_size("blk")
    n_dev = arrow_count * nb
    block_rows = diag_values.shape[0]
    capacity = rows // nb + max(rows // (2 * nb), 1)
    cap = (capacity + 15) // 16 * 16
    dot = functools.partial(jnp.dot, preferred_element_type=jnp.float32)
    x, x_head, select, select_head, plane_rank = gather_blocks(features, positions, nb, cap, block_rows)
    inside = (positions // block_rows)[None] == jnp.arange(nb, dtype=jnp.int32)[:, None, None]
    inside = inside.reshape(n_dev, rows)
    before = (jnp.arange(rows)[:, None] < jnp.arange(rows)[None, :]).astype(jnp.bfloat16)
    rank = jnp.where(inside, dot(inside.astype(jnp.bfloat16), before), -1.0).astype(jnp.int32)
    pick = (rank.T[:, :, None] == jnp.arange(cap, dtype=jnp.int32)[None, None, :]).astype(jnp.bfloat16)
    pick = pick.reshape(rows, n_dev * cap)
    group = arrow_count * cap
    arm_pick = jnp.pad(pick[:, :group], ((0, 0), (0, (group // 128 + 1) * 128 - group)))
    masks = jnp.repeat(tile_masks, block_rows // tile_masks.shape[2], axis=2).astype(jnp.float32)
    masks = jnp.stack([masks[2], masks[0], masks[1]])
    aggregate = return_rows(x, x_head, select, select_head, pick, arm_pick, masks,
                            diag_values, column_values, row_values, nb, cap)
    joined = jnp.concatenate([features, aggregate], axis=1)
    hidden = jax.nn.silu(dot(joined, up_weight)).astype(jnp.bfloat16)
    return dot(hidden, down_weight).astype(jnp.bfloat16)


def solution(mesh):
    in_specs = (
        P(("arrow", "blk"), None),
        P(None, ("arrow", "blk")),
        P("arrow", "blk"),
        P("arrow", "blk"),
        P("arrow", "blk"),
        P(None, "arrow", "blk"),
        P(),
        P(),
    )
    out_specs = P(("arrow", "blk"), None)
    return jax.shard_map(body, mesh=mesh, in_specs=in_specs, out_specs=out_specs, check_vma=False)
```

```python
import functools

import jax
import jax.numpy as jnp
from jax import lax
from jax.experimental import pallas as pl
from jax.experimental.pallas import tpu as pltpu
from jax.sharding import PartitionSpec as P

MESH = pl.DeviceIdType.MESH


def gather_kernel(dims, features_ref, positions_ref, x_ref, xh_ref, st_ref, sth_ref, rank_ref, held,
                  digit_buf, packed, place_col, place_row, zs, zr, xs, xr, ys, yr, dxs, dxr, dys, dyr, cs, cr, own_sem):
    nb, rows, cap, block_rows = dims
    lines = nb // 2
    n_dev = 4 * nb
    width = features_ref.shape[1]
    padded = rows + 16
    f32, bf16 = jnp.float32, jnp.bfloat16
    half = (padded // 2 + 15) // 16 * 16
    a, b = lax.axis_index("arrow"), lax.axis_index("blk")
    ao, c, bo, bi = a // 2, a % 2, b // 2, b % 2
    up, down = (a, b + 2), (a, b - 2)
    across = ((1 - ao) * 2 + c, b)
    beside = (a, bo * 2 + 1 - bi)
    core = (ao * 2 + 1 - c, b)

    def column(ao_, c_, bi_):
        return (ao_ * 2 + c_) * 2 + bi_

    mine = column(ao, c, bi)
    x_col = column(1 - ao, c, bi)
    y_col = column(ao, c, 1 - bi)
    d_col = column(1 - ao, c, 1 - bi)
    cols = (mine, x_col, y_col, d_col)
    other = (column(ao, 1 - c, bi), column(1 - ao, 1 - c, bi), column(ao, 1 - c, 1 - bi),
             column(1 - ao, 1 - c, 1 - bi))
    whole_rows = pl.ds(0, padded)
    top, low = pl.ds(0, half), pl.ds(half, padded - half)

    def send(col, k, part, ssem, rsem, device):
        view = held.at[col, k, part]
        return pltpu.make_async_remote_copy(
            src_ref=view, dst_ref=view, send_sem=ssem, recv_sem=rsem,
            device_id=device, device_id_type=MESH)

    def z_up(k):
        return send(mine, k, whole_rows, zs.at[0, k], zr.at[k], up)

    def z_down(k):
        return send(mine, k, whole_rows, zs.at[1, k], zr.at[k], down)

    def x_send(k):
        return send(mine, k, whole_rows, xs.at[k], xr.at[k], across)

    def y_send(k):
        return send(mine, k, whole_rows, ys.at[k], yr.at[k], beside)

    def dy_send(k):
        return send(x_col, k, top, dys.at[k], dyr.at[k], beside)

    def dx_send(k):
        return send(y_col, k, low, dxs.at[k], dxr.at[k], across)

    def core_send(kind, k):
        return send(cols[kind], k, whole_rows, cs.at[kind, k], cr.at[kind, k], core)

    own = pltpu.make_async_copy(features_ref, held.at[mine, bo, pl.ds(0, rows)], own_sem)
    own.start()
    place = positions_ref[...]
    digit_buf[...] = jnp.zeros(digit_buf.shape, f32)
    digit_buf[pl.ds(0, 4), pl.ds(0, rows)] = (place // 256).astype(f32)
    digit_buf[pl.ds(4, 4), pl.ds(0, rows)] = (place % 256).astype(f32)
    held[mine, bo, pl.ds(rows, 16), :] = digit_buf[...].astype(bf16)
    barrier = pltpu.get_barrier_semaphore()
    for device in (across, beside, core):
        pl.semaphore_signal(barrier, inc=1, device_id=device, device_id_type=MESH)

    @pl.when(bo < lines - 1)
    def _():
        pl.semaphore_signal(barrier, inc=1, device_id=up, device_id_type=MESH)

    @pl.when(bo > 0)
    def _():
        pl.semaphore_signal(barrier, inc=1, device_id=down, device_id_type=MESH)

    ends = (bo < lines - 1).astype(jnp.int32) + (bo > 0).astype(jnp.int32)
    pl.semaphore_wait(barrier, 3 + ends)

    own.wait()

    q_row = lax.broadcasted_iota(jnp.int32, (16, 16), 0)
    q_lane = lax.broadcasted_iota(jnp.int32, (16, 16), 1)
    before = (lax.broadcasted_iota(jnp.int32, (rows, rows), 0)
              < lax.broadcasted_iota(jnp.int32, (rows, rows), 1)).astype(f32).astype(bf16)

    def ranks(digits, arrow, base):
        weight = jnp.where(q_lane == arrow, 256.0, jnp.where(q_lane == arrow + 4, 1.0, 0.0)).astype(bf16)
        place = jnp.dot(weight, digits, preferred_element_type=f32)
        inside = (place >= base) & (place < base + block_rows)
        count = jnp.dot(jnp.where(inside, 1.0, 0.0).astype(bf16), before, preferred_element_type=f32)
        return place - base, jnp.where(inside, count, -1.0)

    slot_id = lax.broadcasted_iota(jnp.int32, (cap, rows), 0).astype(f32)
    lane_id = lax.broadcasted_iota(jnp.int32, (cap, block_rows), 1).astype(f32)
    block_base = jnp.where(lax.broadcasted_iota(jnp.int32, (16, rows), 0) == 0,
                           (b * block_rows).astype(f32), 0.0)

    def pack(col, k):
        at = pl.multiple_of(((k * 2 + col % 2) * 4 + col // 2) * cap, 16)
        place, rank = ranks(held[col, k, pl.ds(rows, 16), pl.ds(0, rows)], a, block_base)
        chosen = []
        for kind, out in ((0, st_ref), (1, sth_ref)):
            match = slot_id == rank[kind:kind + 1, :]
            where = jnp.sum(jnp.where(match, place[kind:kind + 1, :] + 1.0, 0.0),
                            axis=1, keepdims=True) - 1.0
            out[pl.ds(at, cap), :] = jnp.where(lane_id == where, 1.0, 0.0).astype(bf16)
            place_col[kind, pl.ds(at, cap), :] = jnp.broadcast_to(where, (cap, 128))
            chosen.append(jnp.where(match, 1.0, 0.0).astype(bf16))
        found = jnp.dot(jnp.concatenate(chosen, axis=0), held[col, k, pl.ds(0, rows), :],
                        preferred_element_type=f32).astype(bf16)
        packed[0, pl.ds(at, cap), :] = found[:cap]
        packed[1, pl.ds(at, cap), :] = found[cap:]

    def step(t, carry):
        for sign in (-1, 1):
            k = bo + sign * t
            ok = (k >= 0) & (k < lines) & (t < lines)
            if sign == 1:
                ok = ok & (t > 0)

            @pl.when(ok)
            def _():
                @pl.when(t > 0)
                def _():
                    send(mine, k, whole_rows, zs.at[0, k], zr.at[k], up).wait_recv()

                @pl.when((k <= bo) & (bo < lines - 1))
                def _():
                    z_up(k).start()

                @pl.when((k >= bo) & (bo > 0))
                def _():
                    z_down(k).start()

                x_send(k).start()
                y_send(k).start()
                core_send(0, k).start()

        for sign in (-1, 1):
            t2 = t - 1
            k2 = bo + sign * t2
            ok2 = (k2 >= 0) & (k2 < lines) & (t2 >= 0) & (t2 < lines)
            if sign == 1:
                ok2 = ok2 & (t2 > 0)

            @pl.when(ok2)
            def _():
                send(x_col, k2, whole_rows, xs.at[k2], xr.at[k2], across).wait_recv()
                dy_send(k2).start()
                core_send(1, k2).start()
                send(y_col, k2, whole_rows, ys.at[k2], yr.at[k2], beside).wait_recv()
                dx_send(k2).start()
                core_send(2, k2).start()

        for sign in (-1, 1):
            t3 = t - 2
            k3 = bo + sign * t3
            ok3 = (k3 >= 0) & (k3 < lines) & (t3 >= 0)
            if sign == 1:
                ok3 = ok3 & (t3 > 0)

            @pl.when(ok3)
            def _():
                send(d_col, k3, top, dys.at[k3], dyr.at[k3], beside).wait_recv()
                send(d_col, k3, low, dxs.at[k3], dxr.at[k3], across).wait_recv()
                core_send(3, k3).start()

        def visit(i, inner):
            sign, kind, far = i % 2 * 2 - 1, i // 2 % 4, i // 8
            late = t - (kind + 1) // 2 - far
            k = bo + sign * late
            ok = (late >= 0) & (late < lines) & (k >= 0) & (k < lines) & ((late > 0) | (sign < 0))
            col = column((ao + kind % 2) % 2, (c + far) % 2, (bi + kind // 2) % 2)

            @pl.when(ok)
            def _():
                @pl.when(far == 1)
                def _():
                    send(col, k, whole_rows, cs.at[kind, k], cr.at[kind, k], core).wait_recv()

                pack(col, k)
            return inner

        lax.fori_loop(0, 16, visit, 0)
        return carry

    lax.fori_loop(0, lines + 3, step, 0)

    q = lax.broadcasted_iota(jnp.int32, (16, rows), 0)
    plane_base = jnp.where(q < 8, (bo * 2 + q % 2) * block_rows, jnp.where(q < 12, 0, -block_rows)).astype(f32)
    plane_arrow = jnp.where(q_row < 8, q_row // 2, q_row % 4)

    def plane_ranks(k, carry):
        rank_ref[k] = ranks(held[mine, k, pl.ds(rows, 16), pl.ds(0, rows)], plane_arrow, plane_base)[1]
        return carry

    lax.fori_loop(0, lines, plane_ranks, 0)

    def turn(i, carry):
        part = pl.ds(pl.multiple_of(i * 128, 128), 128)
        for kind in range(2):
            place_row[kind, :, part] = place_col[kind, part, :].T[0:8, :]
        return carry

    lax.fori_loop(0, place_row.shape[2] // 128, turn, 0)
    piece = 256
    row_id = lax.broadcasted_iota(jnp.int32, (piece, place_row.shape[2]), 0).astype(f32)

    def unpack(i, carry):
        part = pl.ds(pl.multiple_of(i * piece, piece), piece)
        for kind, out in ((0, x_ref), (1, xh_ref)):
            target = place_row[kind, 0:1, :] - (i * piece).astype(f32)
            select = jnp.where(row_id == target, 1.0, 0.0).astype(bf16)
            out[part, :] = jnp.dot(select, packed[kind], preferred_element_type=f32).astype(bf16)
        return carry

    lax.fori_loop(0, block_rows // piece, unpack, 0)

    def drain(k, carry):
        @pl.when((k <= bo) & (bo < lines - 1))
        def _():
            z_up(k).wait_send()

        @pl.when((k >= bo) & (bo > 0))
        def _():
            z_down(k).wait_send()

        x_send(k).wait_send()
        y_send(k).wait_send()
        dy_send(k).wait_send()
        dx_send(k).wait_send()
        for kind in range(4):
            core_send(kind, k).wait_send()
        return carry

    lax.fori_loop(0, lines, drain, 0)


def gather_blocks(features, positions, nb, cap, block_rows):
    rows, width = features.shape
    n_dev = 4 * nb
    lines = nb // 2
    padded = rows + 16
    slots = n_dev * cap
    dma = pltpu.SemaphoreType.DMA
    vmem = pl.BlockSpec(memory_space=pltpu.VMEM)
    bf16 = jnp.bfloat16
    return pl.pallas_call(
        functools.partial(gather_kernel, (nb, rows, cap, block_rows)),
        out_shape=(
            jax.ShapeDtypeStruct((block_rows, width), bf16),
            jax.ShapeDtypeStruct((block_rows, width), bf16),
            jax.ShapeDtypeStruct((slots, block_rows), bf16),
            jax.ShapeDtypeStruct((slots, block_rows), bf16),
            jax.ShapeDtypeStruct((lines, 16, rows), jnp.float32),
        ),
        in_specs=[vmem, vmem],
        out_specs=(vmem,) * 5,
        scratch_shapes=[
            pltpu.VMEM((8, lines, padded, width), bf16),
            pltpu.VMEM((16, width), jnp.float32),
            pltpu.VMEM((2, slots, width), bf16),
            pltpu.VMEM((2, slots, 128), jnp.float32),
            pltpu.VMEM((2, 8, slots), jnp.float32),
            dma((2, lines)), dma((lines,)),
            dma((lines,)), dma((lines,)), dma((lines,)), dma((lines,)),
            dma((lines,)), dma((lines,)), dma((lines,)), dma((lines,)),
            dma((4, lines)), dma((4, lines)), dma(()),
        ],
        compiler_params=pltpu.CompilerParams(
            collective_id=0, has_side_effects=True, vmem_limit_bytes=60 * 2**20),
        name="gather_blocks",
    )(features, positions)


def return_kernel(dims, x_ref, xh_ref, st_ref, sth_ref, rank_ref, tiles_ref, diag_hbm, column_hbm,
                  row_hbm, agg_ref, blocks, masks, arm, results, outgoing, incoming, partial, column_in,
                  load_sem, psend, precv, zsend, zrecv):
    nb, cap = dims
    lines = nb // 2
    block_rows, width = x_ref.shape
    a, b = lax.axis_index("arrow"), lax.axis_index("blk")
    bo, bi = b // 2, b % 2
    me = bi * 4 + a
    f32, bf16 = jnp.float32, jnp.bfloat16
    edge = tiles_ref.shape[1]
    tile = block_rows // edge

    loads = [pltpu.make_async_copy(ref, blocks.at[i], load_sem.at[i])
             for i, ref in enumerate((diag_hbm, column_hbm, row_hbm))]
    for load in loads:
        load.start()

    barrier = pltpu.get_barrier_semaphore()

    def greet(to, carry):
        @pl.when(to != me)
        def _():
            pl.semaphore_signal(barrier, inc=1, device_id=(to % 4, bo * 2 + to // 4),
                                device_id_type=MESH)
        return carry

    def greet_column(k, carry):
        @pl.when(k != bo)
        def _():
            pl.semaphore_signal(barrier, inc=1, device_id=(a, k * 2 + bi), device_id_type=MESH)
        return carry

    lax.fori_loop(0, 8, greet, 0)
    lax.fori_loop(0, lines, greet_column, 0)
    spread = (lax.broadcasted_iota(jnp.int32, (edge, block_rows), 1) // tile
              == lax.broadcasted_iota(jnp.int32, (edge, block_rows), 0)).astype(f32)
    for kind in range(3):
        masks[kind] = jnp.dot(tiles_ref[kind].astype(f32), spread, preferred_element_type=f32)

    def masked(kind, i):
        rows = pl.ds(pl.multiple_of(i * tile, tile), tile)
        return blocks[kind, rows, :] * masks[kind, pl.ds(i, 1), :].astype(bf16)

    for load in loads:
        load.wait()

    def block_tile(i, carry):
        rows = pl.ds(pl.multiple_of(i * tile, tile), tile)
        arm[rows, :] = jnp.dot(masked(2, i), x_ref[...], preferred_element_type=f32).astype(bf16)
        results[rows, :] = (
            jnp.dot(masked(0, i), x_ref[...], preferred_element_type=f32)
            + jnp.dot(masked(1, i), xh_ref[...], preferred_element_type=f32)).astype(bf16)
        return carry

    lax.fori_loop(0, edge, block_tile, 0)
    pl.semaphore_wait(barrier, 7 + lines - 1)

    def plane_copy(k, to, frm):
        return pltpu.make_async_remote_copy(
            src_ref=outgoing.at[k, to], dst_ref=incoming.at[k, frm], send_sem=psend.at[k, to],
            recv_sem=precv.at[k, frm], device_id=(to % 4, bo * 2 + to // 4), device_id_type=MESH)

    def column_copy(to, frm):
        return pltpu.make_async_remote_copy(
            src_ref=partial.at[to], dst_ref=column_in.at[frm], send_sem=zsend.at[to],
            recv_sem=zrecv.at[frm], device_id=(a, to * 2 + bi), device_id_type=MESH)

    def far_first(body):
        def step(i, carry):
            late = lines - 1 - i // 2
            k = bo + (i % 2 * 2 - 1) * late
            pl.when((k >= 0) & (k < lines) & ((late > 0) | (i % 2 == 0)))(functools.partial(body, k))
            return carry
        lax.fori_loop(0, 2 * lines, step, 0)

    def send_chunk(k):
        chunk = 8 * cap
        rows = pl.ds(pl.multiple_of(k * chunk, 16), chunk)
        for kind, select, values in ((0, st_ref, results), (1, sth_ref, arm)):
            found = jnp.dot(select[rows, :], values[...], preferred_element_type=f32).astype(bf16)
            outgoing[k, :, pl.ds(kind * cap, cap), :] = found.reshape(8, cap, width)

        def one(to, carry):
            @pl.when(to != me)
            def _():
                plane_copy(k, to, me).start()
            return carry

        lax.fori_loop(0, 8, one, 0)
        incoming[k, me] = outgoing[k, me]

    far_first(send_chunk)
    lane = lax.broadcasted_iota(jnp.int32, (16, 16 * cap), 1)
    frm = lane // (2 * cap)
    source = jnp.where(lane // cap % 2 == 0, frm % 4 * 2 + frm // 4, 8 + frm % 4)
    expand = (lax.broadcasted_iota(jnp.int32, (16, 16 * cap), 0) == source).astype(f32).astype(bf16)
    slot = (lax.broadcasted_iota(jnp.int32, (1, 16 * cap), 1) % cap).astype(f32)

    def sum_chunk(k):
        held = lax.dot_general(rank_ref[k].astype(bf16), expand, (((0,), (0,)), ((), ())),
                               preferred_element_type=f32)
        gather = jnp.where(held == slot, 1.0, 0.0).astype(bf16)

        def one(frm, carry):
            @pl.when(frm != me)
            def _():
                plane_copy(k, me, frm).wait_recv()
            return carry

        lax.fori_loop(0, 8, one, 0)
        partial[k] = jnp.dot(gather, incoming[k].reshape(16 * cap, width),
                             preferred_element_type=f32).astype(bf16)

        @pl.when(k != bo)
        def _():
            column_copy(k, bo).start()

    far_first(sum_chunk)

    def drain(k, carry):
        def one(to, inner):
            @pl.when(to != me)
            def _():
                plane_copy(k, to, me).wait_send()
            return inner

        lax.fori_loop(0, 8, one, 0)

        @pl.when(k != bo)
        def _():
            column_copy(k, bo).wait_send()
            column_copy(bo, k).wait_recv()
        return carry

    lax.fori_loop(0, lines, drain, 0)
    column_in[bo] = partial[bo]
    agg_ref[...] = jnp.sum(column_in[...].astype(f32), axis=0).astype(bf16)


def return_rows(x, xh, select, select_head, plane_rank, tiles, diag, column, row, nb, cap):
    block_rows, width = x.shape
    lines, _, rows = plane_rank.shape
    dma = pltpu.SemaphoreType.DMA
    vmem = pl.BlockSpec(memory_space=pltpu.VMEM)
    hbm = pl.BlockSpec(memory_space=pl.ANY)
    bf16 = jnp.bfloat16
    return pl.pallas_call(
        functools.partial(return_kernel, (nb, cap)),
        out_shape=jax.ShapeDtypeStruct((rows, width), bf16),
        in_specs=[vmem] * 6 + [hbm] * 3,
        out_specs=vmem,
        scratch_shapes=[
            pltpu.VMEM((3, block_rows, block_rows), bf16),
            pltpu.VMEM((3, tiles.shape[1], block_rows), jnp.float32),
            pltpu.VMEM((block_rows, width), bf16),
            pltpu.VMEM((block_rows, width), bf16),
            pltpu.VMEM((lines, 8, 2 * cap, width), bf16),
            pltpu.VMEM((lines, 8, 2 * cap, width), bf16),
            pltpu.VMEM((lines, rows, width), bf16),
            pltpu.VMEM((lines, rows, width), bf16),
            dma((3,)), dma((lines, 8)), dma((lines, 8)), dma((lines,)), dma((lines,)),
        ],
        compiler_params=pltpu.CompilerParams(
            collective_id=1, has_side_effects=True, vmem_limit_bytes=56 * 2**20),
        name="return_rows",
    )(x, xh, select, select_head, plane_rank, tiles, diag, column, row)


def body(
    features, positions, diag_values, column_values, row_values, tile_masks, up_weight, down_weight
):
    rows = features.shape[0]
    nb = lax.axis_size("blk")
    block_rows = diag_values.shape[0]
    capacity = rows // nb + max(rows // (2 * nb), 1)
    cap = (capacity + 15) // 16 * 16
    dot = functools.partial(jnp.dot, preferred_element_type=jnp.float32)
    x, x_head, select, select_head, plane_rank = gather_blocks(
        features, positions, nb, cap, block_rows)
    aggregate = return_rows(x, x_head, select, select_head, plane_rank, tile_masks,
                            diag_values, column_values, row_values, nb, cap)
    joined = jnp.concatenate([features, aggregate], axis=1)
    hidden = jax.nn.silu(dot(joined, up_weight)).astype(jnp.bfloat16)
    return dot(hidden, down_weight).astype(jnp.bfloat16)


def solution(mesh):
    in_specs = (
        P(("arrow", "blk"), None),
        P(None, ("arrow", "blk")),
        P("arrow", "blk"),
        P("arrow", "blk"),
        P("arrow", "blk"),
        P(None, "arrow", "blk"),
        P(),
        P(),
    )
    out_specs = P(("arrow", "blk"), None)
    return jax.shard_map(body, mesh=mesh, in_specs=in_specs, out_specs=out_specs, check_vma=False)
```

```python
import functools

import jax
import jax.numpy as jnp
from jax import lax
from jax.experimental import pallas as pl
from jax.experimental.pallas import tpu as pltpu
from jax.sharding import PartitionSpec as P

MESH = pl.DeviceIdType.MESH


def gather_kernel(dims, features_ref, positions_ref, x_ref, xh_ref, st_ref, sth_ref, rank_ref, held,
                  digit_buf, packed, sums, place_col, place_row, zs, zr, xs, xr, ys, yr, dxs, dxr, dys, dyr, cs, cr, own_sem):
    nb, rows, cap, block_rows = dims
    lines = nb // 2
    n_dev = 4 * nb
    width = features_ref.shape[1]
    padded = rows + 16
    f32, bf16 = jnp.float32, jnp.bfloat16
    half = (padded // 2 + 15) // 16 * 16
    a, b = lax.axis_index("arrow"), lax.axis_index("blk")
    ao, c, bo, bi = a // 2, a % 2, b // 2, b % 2
    up, down = (a, b + 2), (a, b - 2)
    across = ((1 - ao) * 2 + c, b)
    beside = (a, bo * 2 + 1 - bi)
    core = (ao * 2 + 1 - c, b)

    def column(ao_, c_, bi_):
        return (ao_ * 2 + c_) * 2 + bi_

    mine = column(ao, c, bi)
    x_col = column(1 - ao, c, bi)
    y_col = column(ao, c, 1 - bi)
    d_col = column(1 - ao, c, 1 - bi)
    cols = (mine, x_col, y_col, d_col)
    other = (column(ao, 1 - c, bi), column(1 - ao, 1 - c, bi), column(ao, 1 - c, 1 - bi),
             column(1 - ao, 1 - c, 1 - bi))
    whole_rows = pl.ds(0, padded)
    top, low = pl.ds(0, half), pl.ds(half, padded - half)

    def send(col, k, part, ssem, rsem, device):
        view = held.at[col, k, part]
        return pltpu.make_async_remote_copy(
            src_ref=view, dst_ref=view, send_sem=ssem, recv_sem=rsem,
            device_id=device, device_id_type=MESH)

    def z_up(k):
        return send(mine, k, whole_rows, zs.at[0, k], zr.at[k], up)

    def z_down(k):
        return send(mine, k, whole_rows, zs.at[1, k], zr.at[k], down)

    def x_send(k):
        return send(mine, k, whole_rows, xs.at[k], xr.at[k], across)

    def y_send(k):
        return send(mine, k, whole_rows, ys.at[k], yr.at[k], beside)

    def dy_send(k):
        return send(x_col, k, top, dys.at[k], dyr.at[k], beside)

    def dx_send(k):
        return send(y_col, k, low, dxs.at[k], dxr.at[k], across)

    def core_send(kind, k):
        return send(cols[kind], k, whole_rows, cs.at[kind, k], cr.at[kind, k], core)

    own = pltpu.make_async_copy(features_ref, held.at[mine, bo, pl.ds(0, rows)], own_sem)
    own.start()
    place = positions_ref[...]
    digit_buf[...] = jnp.zeros(digit_buf.shape, f32)
    digit_buf[pl.ds(0, 4), pl.ds(0, rows)] = (place // 256).astype(f32)
    digit_buf[pl.ds(4, 4), pl.ds(0, rows)] = (place % 256).astype(f32)
    held[mine, bo, pl.ds(rows, 16), :] = digit_buf[...].astype(bf16)
    barrier = pltpu.get_barrier_semaphore()
    for device in (across, beside, core):
        pl.semaphore_signal(barrier, inc=1, device_id=device, device_id_type=MESH)

    @pl.when(bo < lines - 1)
    def _():
        pl.semaphore_signal(barrier, inc=1, device_id=up, device_id_type=MESH)

    @pl.when(bo > 0)
    def _():
        pl.semaphore_signal(barrier, inc=1, device_id=down, device_id_type=MESH)

    sums[...] = jnp.zeros(sums.shape, f32)
    ends = (bo < lines - 1).astype(jnp.int32) + (bo > 0).astype(jnp.int32)
    pl.semaphore_wait(barrier, 3 + ends)

    own.wait()

    q_row = lax.broadcasted_iota(jnp.int32, (16, 16), 0)
    q_lane = lax.broadcasted_iota(jnp.int32, (16, 16), 1)
    before = (lax.broadcasted_iota(jnp.int32, (rows, rows), 0)
              < lax.broadcasted_iota(jnp.int32, (rows, rows), 1)).astype(f32).astype(bf16)

    def ranks(digits, arrow, base):
        weight = jnp.where(q_lane == arrow, 256.0, jnp.where(q_lane == arrow + 4, 1.0, 0.0)).astype(bf16)
        place = jnp.dot(weight, digits, preferred_element_type=f32)
        inside = (place >= base) & (place < base + block_rows)
        count = jnp.dot(jnp.where(inside, 1.0, 0.0).astype(bf16), before, preferred_element_type=f32)
        return place - base, jnp.where(inside, count, -1.0)

    slot_id = lax.broadcasted_iota(jnp.int32, (cap, rows), 0).astype(f32)
    lane_id = lax.broadcasted_iota(jnp.int32, (cap, block_rows), 1).astype(f32)
    block_base = jnp.where(lax.broadcasted_iota(jnp.int32, (16, rows), 0) == 0,
                           (b * block_rows).astype(f32), 0.0)

    def pack(col, k):
        at = pl.multiple_of(((k * 2 + col % 2) * 4 + col // 2) * cap, 16)
        place, rank = ranks(held[col, k, pl.ds(rows, 16), pl.ds(0, rows)], a, block_base)
        chosen = []
        for kind, out in ((0, st_ref), (1, sth_ref)):
            match = slot_id == rank[kind:kind + 1, :]
            where = jnp.sum(jnp.where(match, place[kind:kind + 1, :] + 1.0, 0.0),
                            axis=1, keepdims=True) - 1.0
            out[pl.ds(at, cap), :] = jnp.where(lane_id == where, 1.0, 0.0).astype(bf16)
            place_col[kind, pl.ds(at, cap), :] = jnp.broadcast_to(where, (cap, 128))
            chosen.append(jnp.where(match, 1.0, 0.0).astype(bf16))
        found = jnp.dot(jnp.concatenate(chosen, axis=0), held[col, k, pl.ds(0, rows), :],
                        preferred_element_type=f32).astype(bf16)
        packed[0, pl.ds(at, cap), :] = found[:cap]
        packed[1, pl.ds(at, cap), :] = found[cap:]

    chunk = 8 * cap
    piece = 256
    row_id = lax.broadcasted_iota(jnp.int32, (piece, chunk), 0).astype(f32)

    def unpack(k):
        start = k * chunk
        for kind in range(2):
            for i in range(chunk // 128):
                part = pl.ds(pl.multiple_of(start + i * 128, 128), 128)
                place_row[kind, :, pl.ds(i * 128, 128)] = place_col[kind, part, :].T[0:8, :]

        def one(i, carry):
            part = pl.ds(pl.multiple_of(i * piece, piece), piece)
            slots = pl.ds(pl.multiple_of(start, 128), chunk)
            for kind in range(2):
                target = place_row[kind, 0:1, :] - (i * piece).astype(f32)
                select = jnp.where(row_id == target, 1.0, 0.0).astype(bf16)
                sums[kind, part, :] += jnp.dot(select, packed[kind, slots, :], preferred_element_type=f32)
            return carry

        lax.fori_loop(0, block_rows // piece, one, 0)

    def step(t, carry):
        for sign in (-1, 1):
            k = bo + sign * t
            ok = (k >= 0) & (k < lines) & (t < lines)
            if sign == 1:
                ok = ok & (t > 0)

            @pl.when(ok)
            def _():
                @pl.when(t > 0)
                def _():
                    send(mine, k, whole_rows, zs.at[0, k], zr.at[k], up).wait_recv()

                @pl.when((k <= bo) & (bo < lines - 1))
                def _():
                    z_up(k).start()

                @pl.when((k >= bo) & (bo > 0))
                def _():
                    z_down(k).start()

                x_send(k).start()
                y_send(k).start()
                core_send(0, k).start()

        for sign in (-1, 1):
            t2 = t - 1
            k2 = bo + sign * t2
            ok2 = (k2 >= 0) & (k2 < lines) & (t2 >= 0) & (t2 < lines)
            if sign == 1:
                ok2 = ok2 & (t2 > 0)

            @pl.when(ok2)
            def _():
                send(x_col, k2, whole_rows, xs.at[k2], xr.at[k2], across).wait_recv()
                dy_send(k2).start()
                core_send(1, k2).start()
                send(y_col, k2, whole_rows, ys.at[k2], yr.at[k2], beside).wait_recv()
                dx_send(k2).start()
                core_send(2, k2).start()

        for sign in (-1, 1):
            t3 = t - 2
            k3 = bo + sign * t3
            ok3 = (k3 >= 0) & (k3 < lines) & (t3 >= 0)
            if sign == 1:
                ok3 = ok3 & (t3 > 0)

            @pl.when(ok3)
            def _():
                send(d_col, k3, top, dys.at[k3], dyr.at[k3], beside).wait_recv()
                send(d_col, k3, low, dxs.at[k3], dxr.at[k3], across).wait_recv()
                core_send(3, k3).start()

        def visit(i, inner):
            sign, kind, far = i % 2 * 2 - 1, i // 2 % 4, i // 8
            late = t - (kind + 1) // 2 - far
            k = bo + sign * late
            ok = (late >= 0) & (late < lines) & (k >= 0) & (k < lines) & ((late > 0) | (sign < 0))
            col = column((ao + kind % 2) % 2, (c + far) % 2, (bi + kind // 2) % 2)

            @pl.when(ok)
            def _():
                @pl.when(far == 1)
                def _():
                    send(col, k, whole_rows, cs.at[kind, k], cr.at[kind, k], core).wait_recv()

                pack(col, k)
            return inner

        lax.fori_loop(0, 16, visit, 0)

        def finish(i, inner):
            late = t - 3
            k = bo + (i * 2 - 1) * late
            ok = (late >= 0) & (k >= 0) & (k < lines) & ((late > 0) | (i == 0))
            pl.when(ok)(functools.partial(unpack, k))
            return inner

        lax.fori_loop(0, 2, finish, 0)
        return carry

    lax.fori_loop(0, lines + 3, step, 0)

    q = lax.broadcasted_iota(jnp.int32, (16, rows), 0)
    plane_base = jnp.where(q < 8, (bo * 2 + q % 2) * block_rows, jnp.where(q < 12, 0, -block_rows)).astype(f32)
    plane_arrow = jnp.where(q_row < 8, q_row // 2, q_row % 4)

    def plane_ranks(k, carry):
        rank_ref[k] = ranks(held[mine, k, pl.ds(rows, 16), pl.ds(0, rows)], plane_arrow, plane_base)[1]
        return carry

    lax.fori_loop(0, lines, plane_ranks, 0)

    x_ref[...] = sums[0].astype(bf16)
    xh_ref[...] = sums[1].astype(bf16)

    def drain(k, carry):
        @pl.when((k <= bo) & (bo < lines - 1))
        def _():
            z_up(k).wait_send()

        @pl.when((k >= bo) & (bo > 0))
        def _():
            z_down(k).wait_send()

        x_send(k).wait_send()
        y_send(k).wait_send()
        dy_send(k).wait_send()
        dx_send(k).wait_send()
        for kind in range(4):
            core_send(kind, k).wait_send()
        return carry

    lax.fori_loop(0, lines, drain, 0)


def gather_blocks(features, positions, nb, cap, block_rows):
    rows, width = features.shape
    n_dev = 4 * nb
    lines = nb // 2
    padded = rows + 16
    slots = n_dev * cap
    dma = pltpu.SemaphoreType.DMA
    vmem = pl.BlockSpec(memory_space=pltpu.VMEM)
    bf16 = jnp.bfloat16
    return pl.pallas_call(
        functools.partial(gather_kernel, (nb, rows, cap, block_rows)),
        out_shape=(
            jax.ShapeDtypeStruct((block_rows, width), bf16),
            jax.ShapeDtypeStruct((block_rows, width), bf16),
            jax.ShapeDtypeStruct((slots, block_rows), bf16),
            jax.ShapeDtypeStruct((slots, block_rows), bf16),
            jax.ShapeDtypeStruct((lines, 16, rows), jnp.float32),
        ),
        in_specs=[vmem, vmem],
        out_specs=(vmem,) * 5,
        scratch_shapes=[
            pltpu.VMEM((8, lines, padded, width), bf16),
            pltpu.VMEM((16, width), jnp.float32),
            pltpu.VMEM((2, slots, width), bf16),
            pltpu.VMEM((2, block_rows, width), jnp.float32),
            pltpu.VMEM((2, slots, 128), jnp.float32),
            pltpu.VMEM((2, 8, 8 * cap), jnp.float32),
            dma((2, lines)), dma((lines,)),
            dma((lines,)), dma((lines,)), dma((lines,)), dma((lines,)),
            dma((lines,)), dma((lines,)), dma((lines,)), dma((lines,)),
            dma((4, lines)), dma((4, lines)), dma(()),
        ],
        compiler_params=pltpu.CompilerParams(
            collective_id=0, has_side_effects=True, vmem_limit_bytes=60 * 2**20),
        name="gather_blocks",
    )(features, positions)


def return_kernel(dims, x_ref, xh_ref, st_ref, sth_ref, rank_ref, tiles_ref, features_ref, diag_hbm,
                  column_hbm, row_hbm, up_hbm, down_hbm, out_ref, blocks, up_weight, down_weight, early,
                  acc, masks, arm, results, outgoing, incoming, partial, column_in, load_sem, psend, precv, zsend, zrecv):
    nb, cap = dims
    lines = nb // 2
    block_rows, width = x_ref.shape
    a, b = lax.axis_index("arrow"), lax.axis_index("blk")
    bo, bi = b // 2, b % 2
    me = bi * 4 + a
    f32, bf16 = jnp.float32, jnp.bfloat16
    edge = tiles_ref.shape[1]
    tile = block_rows // edge

    loads = [pltpu.make_async_copy(ref, blocks.at[i], load_sem.at[i])
             for i, ref in enumerate((diag_hbm, column_hbm, row_hbm))]
    loads.append(pltpu.make_async_copy(up_hbm, up_weight, load_sem.at[3]))
    loads.append(pltpu.make_async_copy(down_hbm, down_weight, load_sem.at[4]))
    for load in loads:
        load.start()

    barrier = pltpu.get_barrier_semaphore()

    def greet(to, carry):
        @pl.when(to != me)
        def _():
            pl.semaphore_signal(barrier, inc=1, device_id=(to % 4, bo * 2 + to // 4),
                                device_id_type=MESH)
        return carry

    def greet_column(k, carry):
        @pl.when(k != bo)
        def _():
            pl.semaphore_signal(barrier, inc=1, device_id=(a, k * 2 + bi), device_id_type=MESH)
        return carry

    lax.fori_loop(0, 8, greet, 0)
    lax.fori_loop(0, lines, greet_column, 0)
    spread = (lax.broadcasted_iota(jnp.int32, (edge, block_rows), 1) // tile
              == lax.broadcasted_iota(jnp.int32, (edge, block_rows), 0)).astype(f32)
    for kind in range(3):
        masks[kind] = jnp.dot(tiles_ref[kind].astype(f32), spread, preferred_element_type=f32)

    def masked(kind, i):
        rows = pl.ds(pl.multiple_of(i * tile, tile), tile)
        return blocks[kind, rows, :] * masks[kind, pl.ds(i, 1), :].astype(bf16)

    for load in loads[:3]:
        load.wait()

    def block_tile(i, carry):
        rows = pl.ds(pl.multiple_of(i * tile, tile), tile)
        arm[rows, :] = jnp.dot(masked(2, i), x_ref[...], preferred_element_type=f32).astype(bf16)
        results[rows, :] = (
            jnp.dot(masked(0, i), x_ref[...], preferred_element_type=f32)
            + jnp.dot(masked(1, i), xh_ref[...], preferred_element_type=f32)).astype(bf16)
        return carry

    lax.fori_loop(0, edge, block_tile, 0)
    pl.semaphore_wait(barrier, 7 + lines - 1)

    def plane_copy(k, to, frm):
        return pltpu.make_async_remote_copy(
            src_ref=outgoing.at[k, to], dst_ref=incoming.at[k, frm], send_sem=psend.at[k, to],
            recv_sem=precv.at[k, frm], device_id=(to % 4, bo * 2 + to // 4), device_id_type=MESH)

    def column_copy(to, frm):
        return pltpu.make_async_remote_copy(
            src_ref=partial.at[to], dst_ref=column_in.at[frm], send_sem=zsend.at[to],
            recv_sem=zrecv.at[frm], device_id=(a, to * 2 + bi), device_id_type=MESH)

    def far_first(body):
        def step(i, carry):
            late = lines - 1 - i // 2
            k = bo + (i % 2 * 2 - 1) * late
            pl.when((k >= 0) & (k < lines) & ((late > 0) | (i % 2 == 0)))(functools.partial(body, k))
            return carry
        lax.fori_loop(0, 2 * lines, step, 0)

    def send_chunk(k):
        chunk = 8 * cap
        rows = pl.ds(pl.multiple_of(k * chunk, 16), chunk)
        for kind, select, values in ((0, st_ref, results), (1, sth_ref, arm)):
            found = jnp.dot(select[rows, :], values[...], preferred_element_type=f32).astype(bf16)
            outgoing[k, :, pl.ds(kind * cap, cap), :] = found.reshape(8, cap, width)

        def one(to, carry):
            @pl.when(to != me)
            def _():
                plane_copy(k, to, me).start()
            return carry

        lax.fori_loop(0, 8, one, 0)
        incoming[k, me] = outgoing[k, me]

    far_first(send_chunk)
    loads[3].wait()
    hidden_width = up_weight.shape[1]
    part = 512

    def first_half(i, carry):
        lanes = pl.ds(pl.multiple_of(i * part, part), part)
        early[:, lanes] = jnp.dot(features_ref[...], up_weight[pl.ds(0, width), lanes],
                                  preferred_element_type=f32)
        return carry

    lax.fori_loop(0, hidden_width // part, first_half, 0)
    loads[4].wait()
    lane = lax.broadcasted_iota(jnp.int32, (16, 16 * cap), 1)
    frm = lane // (2 * cap)
    source = jnp.where(lane // cap % 2 == 0, frm % 4 * 2 + frm // 4, 8 + frm % 4)
    expand = (lax.broadcasted_iota(jnp.int32, (16, 16 * cap), 0) == source).astype(f32).astype(bf16)
    slot = (lax.broadcasted_iota(jnp.int32, (1, 16 * cap), 1) % cap).astype(f32)

    def sum_chunk(k):
        held = lax.dot_general(rank_ref[k].astype(bf16), expand, (((0,), (0,)), ((), ())),
                               preferred_element_type=f32)
        gather = jnp.where(held == slot, 1.0, 0.0).astype(bf16)

        def one(frm, carry):
            @pl.when(frm != me)
            def _():
                plane_copy(k, me, frm).wait_recv()
            return carry

        lax.fori_loop(0, 8, one, 0)
        partial[k] = jnp.dot(gather, incoming[k].reshape(16 * cap, width),
                             preferred_element_type=f32).astype(bf16)

        @pl.when(k != bo)
        def _():
            column_copy(k, bo).start()

    far_first(sum_chunk)

    def drain(k, carry):
        def one(to, inner):
            @pl.when(to != me)
            def _():
                plane_copy(k, to, me).wait_send()
            return inner

        lax.fori_loop(0, 8, one, 0)

        @pl.when(k != bo)
        def _():
            column_copy(k, bo).wait_send()
            column_copy(bo, k).wait_recv()
        return carry

    lax.fori_loop(0, lines, drain, 0)
    column_in[bo] = partial[bo]
    aggregate = jnp.sum(column_in[...].astype(f32), axis=0).astype(bf16)
    partial[0] = aggregate
    acc[...] = jnp.zeros(acc.shape, f32)

    def mlp(i, carry):
        lanes = pl.ds(pl.multiple_of(i * part, part), part)
        value = early[:, lanes] + jnp.dot(partial[0], up_weight[pl.ds(width, width), lanes],
                                          preferred_element_type=f32)
        hidden = (value / (1.0 + jnp.exp(-value))).astype(bf16)
        acc[...] += jnp.dot(hidden, down_weight[lanes, :], preferred_element_type=f32)
        return carry

    lax.fori_loop(0, hidden_width // part, mlp, 0)
    out_ref[...] = acc[...].astype(bf16)


def return_rows(x, xh, select, select_head, plane_rank, tiles, features, diag, column, row, up, down,
                nb, cap):
    block_rows, width = x.shape
    lines, _, rows = plane_rank.shape
    dma = pltpu.SemaphoreType.DMA
    vmem = pl.BlockSpec(memory_space=pltpu.VMEM)
    hbm = pl.BlockSpec(memory_space=pl.ANY)
    bf16 = jnp.bfloat16
    return pl.pallas_call(
        functools.partial(return_kernel, (nb, cap)),
        out_shape=jax.ShapeDtypeStruct((rows, width), bf16),
        in_specs=[vmem] * 7 + [hbm] * 5,
        out_specs=vmem,
        scratch_shapes=[
            pltpu.VMEM((3, block_rows, block_rows), bf16),
            pltpu.VMEM(up.shape, bf16),
            pltpu.VMEM(down.shape, bf16),
            pltpu.VMEM((rows, up.shape[1]), jnp.float32),
            pltpu.VMEM((rows, width), jnp.float32),
            pltpu.VMEM((3, tiles.shape[1], block_rows), jnp.float32),
            pltpu.VMEM((block_rows, width), bf16),
            pltpu.VMEM((block_rows, width), bf16),
            pltpu.VMEM((lines, 8, 2 * cap, width), bf16),
            pltpu.VMEM((lines, 8, 2 * cap, width), bf16),
            pltpu.VMEM((lines, rows, width), bf16),
            pltpu.VMEM((lines, rows, width), bf16),
            dma((5,)), dma((lines, 8)), dma((lines, 8)), dma((lines,)), dma((lines,)),
        ],
        compiler_params=pltpu.CompilerParams(
            collective_id=1, has_side_effects=True, vmem_limit_bytes=60 * 2**20),
        name="return_rows",
    )(x, xh, select, select_head, plane_rank, tiles, features, diag, column, row, up, down)


def body(
    features, positions, diag_values, column_values, row_values, tile_masks, up_weight, down_weight
):
    rows = features.shape[0]
    nb = lax.axis_size("blk")
    block_rows = diag_values.shape[0]
    capacity = rows // nb + max(rows // (2 * nb), 1)
    cap = (capacity + 15) // 16 * 16
    x, x_head, select, select_head, plane_rank = gather_blocks(
        features, positions, nb, cap, block_rows)
    return return_rows(x, x_head, select, select_head, plane_rank, tile_masks, features,
                       diag_values, column_values, row_values, up_weight, down_weight, nb, cap)


def solution(mesh):
    in_specs = (
        P(("arrow", "blk"), None),
        P(None, ("arrow", "blk")),
        P("arrow", "blk"),
        P("arrow", "blk"),
        P("arrow", "blk"),
        P(None, "arrow", "blk"),
        P(),
        P(),
    )
    out_specs = P(("arrow", "blk"), None)
    return jax.shard_map(body, mesh=mesh, in_specs=in_specs, out_specs=out_specs, check_vma=False)
```

```python
import functools

import jax
import jax.numpy as jnp
from jax import lax
from jax.experimental import pallas as pl
from jax.experimental.pallas import tpu as pltpu
from jax.sharding import PartitionSpec as P

MESH = pl.DeviceIdType.MESH


def gather_kernel(dims, features_ref, positions_ref, x_ref, xh_ref, st_ref, sth_ref, rank_ref, held,
                  digit_buf, packed, place_col, place_row, zs, zr, xs, xr, ys, yr, dxs, dxr, dys, dyr, cs, cr, own_sem):
    nb, rows, cap, block_rows = dims
    lines = nb // 2
    n_dev = 4 * nb
    width = features_ref.shape[1]
    padded = rows + 16
    f32, bf16 = jnp.float32, jnp.bfloat16
    half = (padded // 2 + 15) // 16 * 16
    a, b = lax.axis_index("arrow"), lax.axis_index("blk")
    ao, c, bo, bi = a // 2, a % 2, b // 2, b % 2
    up, down = (a, b + 2), (a, b - 2)
    across = ((1 - ao) * 2 + c, b)
    beside = (a, bo * 2 + 1 - bi)
    core = (ao * 2 + 1 - c, b)

    def column(ao_, c_, bi_):
        return (ao_ * 2 + c_) * 2 + bi_

    mine = column(ao, c, bi)
    x_col = column(1 - ao, c, bi)
    y_col = column(ao, c, 1 - bi)
    d_col = column(1 - ao, c, 1 - bi)
    cols = (mine, x_col, y_col, d_col)
    other = (column(ao, 1 - c, bi), column(1 - ao, 1 - c, bi), column(ao, 1 - c, 1 - bi),
             column(1 - ao, 1 - c, 1 - bi))
    whole_rows = pl.ds(0, padded)
    top, low = pl.ds(0, half), pl.ds(half, padded - half)

    def send(col, k, part, ssem, rsem, device):
        view = held.at[col, k, part]
        return pltpu.make_async_remote_copy(
            src_ref=view, dst_ref=view, send_sem=ssem, recv_sem=rsem,
            device_id=device, device_id_type=MESH)

    def z_up(k):
        return send(mine, k, whole_rows, zs.at[0, k], zr.at[k], up)

    def z_down(k):
        return send(mine, k, whole_rows, zs.at[1, k], zr.at[k], down)

    def x_send(k):
        return send(mine, k, whole_rows, xs.at[k], xr.at[k], across)

    def y_send(k):
        return send(mine, k, whole_rows, ys.at[k], yr.at[k], beside)

    def dy_send(k):
        return send(x_col, k, top, dys.at[k], dyr.at[k], beside)

    def dx_send(k):
        return send(y_col, k, low, dxs.at[k], dxr.at[k], across)

    def core_send(kind, k):
        return send(cols[kind], k, whole_rows, cs.at[kind, k], cr.at[kind, k], core)

    own = pltpu.make_async_copy(features_ref, held.at[mine, bo, pl.ds(0, rows)], own_sem)
    own.start()
    place = positions_ref[...]
    digit_buf[...] = jnp.zeros(digit_buf.shape, f32)
    digit_buf[pl.ds(0, 4), pl.ds(0, rows)] = (place // 256).astype(f32)
    digit_buf[pl.ds(4, 4), pl.ds(0, rows)] = (place % 256).astype(f32)
    held[mine, bo, pl.ds(rows, 16), :] = digit_buf[...].astype(bf16)
    barrier = pltpu.get_barrier_semaphore()
    for device in (across, beside, core):
        pl.semaphore_signal(barrier, inc=1, device_id=device, device_id_type=MESH)

    @pl.when(bo < lines - 1)
    def _():
        pl.semaphore_signal(barrier, inc=1, device_id=up, device_id_type=MESH)

    @pl.when(bo > 0)
    def _():
        pl.semaphore_signal(barrier, inc=1, device_id=down, device_id_type=MESH)

    ends = (bo < lines - 1).astype(jnp.int32) + (bo > 0).astype(jnp.int32)
    pl.semaphore_wait(barrier, 3 + ends)

    own.wait()

    q_row = lax.broadcasted_iota(jnp.int32, (16, 16), 0)
    q_lane = lax.broadcasted_iota(jnp.int32, (16, 16), 1)
    before = (lax.broadcasted_iota(jnp.int32, (rows, rows), 0)
              < lax.broadcasted_iota(jnp.int32, (rows, rows), 1)).astype(f32).astype(bf16)

    def ranks(digits, arrow, base):
        weight = jnp.where(q_lane == arrow, 256.0, jnp.where(q_lane == arrow + 4, 1.0, 0.0)).astype(bf16)
        place = jnp.dot(weight, digits, preferred_element_type=f32)
        inside = (place >= base) & (place < base + block_rows)
        count = jnp.dot(jnp.where(inside, 1.0, 0.0).astype(bf16), before, preferred_element_type=f32)
        return place - base, jnp.where(inside, count, -1.0)

    slot_id = lax.broadcasted_iota(jnp.int32, (cap, rows), 0).astype(f32)
    lane_id = lax.broadcasted_iota(jnp.int32, (cap, block_rows), 1).astype(f32)
    block_base = jnp.where(lax.broadcasted_iota(jnp.int32, (16, rows), 0) == 0,
                           (b * block_rows).astype(f32), 0.0)

    def pack(col, k):
        at = pl.multiple_of(((k * 2 + col % 2) * 4 + col // 2) * cap, 16)
        place, rank = ranks(held[col, k, pl.ds(rows, 16), pl.ds(0, rows)], a, block_base)
        chosen = []
        for kind, out in ((0, st_ref), (1, sth_ref)):
            match = slot_id == rank[kind:kind + 1, :]
            where = jnp.sum(jnp.where(match, place[kind:kind + 1, :] + 1.0, 0.0),
                            axis=1, keepdims=True) - 1.0
            out[pl.ds(at, cap), :] = jnp.where(lane_id == where, 1.0, 0.0).astype(bf16)
            place_col[kind, pl.ds(at, cap), :] = jnp.broadcast_to(where, (cap, 128))
            chosen.append(jnp.where(match, 1.0, 0.0).astype(bf16))
        found = jnp.dot(jnp.concatenate(chosen, axis=0), held[col, k, pl.ds(0, rows), :],
                        preferred_element_type=f32).astype(bf16)
        packed[0, pl.ds(at, cap), :] = found[:cap]
        packed[1, pl.ds(at, cap), :] = found[cap:]

    def step(t, carry):
        def visit(i, inner):
            sign, kind, far = i % 2 * 2 - 1, i // 2 % 4, i // 8
            late = t - 1 - (kind + 1) // 2 - far
            k = bo + sign * late
            ok = (late >= 0) & (late < lines) & (k >= 0) & (k < lines) & ((late > 0) | (sign < 0))
            col = column((ao + kind % 2) % 2, (c + far) % 2, (bi + kind // 2) % 2)

            @pl.when(ok)
            def _():
                @pl.when(far == 1)
                def _():
                    send(col, k, whole_rows, cs.at[kind, k], cr.at[kind, k], core).wait_recv()

                pack(col, k)
            return inner

        for sign in (-1, 1):
            k = bo + sign * t
            ok = (k >= 0) & (k < lines) & (t < lines)
            if sign == 1:
                ok = ok & (t > 0)

            @pl.when(ok)
            def _():
                @pl.when(t > 0)
                def _():
                    send(mine, k, whole_rows, zs.at[0, k], zr.at[k], up).wait_recv()

                @pl.when((k <= bo) & (bo < lines - 1))
                def _():
                    z_up(k).start()

                @pl.when((k >= bo) & (bo > 0))
                def _():
                    z_down(k).start()

                x_send(k).start()
                y_send(k).start()
                core_send(0, k).start()

        lax.fori_loop(0, 6, visit, 0)
        for sign in (-1, 1):
            t2 = t - 1
            k2 = bo + sign * t2
            ok2 = (k2 >= 0) & (k2 < lines) & (t2 >= 0) & (t2 < lines)
            if sign == 1:
                ok2 = ok2 & (t2 > 0)

            @pl.when(ok2)
            def _():
                send(x_col, k2, whole_rows, xs.at[k2], xr.at[k2], across).wait_recv()
                dy_send(k2).start()
                core_send(1, k2).start()
                send(y_col, k2, whole_rows, ys.at[k2], yr.at[k2], beside).wait_recv()
                dx_send(k2).start()
                core_send(2, k2).start()

        lax.fori_loop(6, 11, visit, 0)
        for sign in (-1, 1):
            t3 = t - 2
            k3 = bo + sign * t3
            ok3 = (k3 >= 0) & (k3 < lines) & (t3 >= 0)
            if sign == 1:
                ok3 = ok3 & (t3 > 0)

            @pl.when(ok3)
            def _():
                send(d_col, k3, top, dys.at[k3], dyr.at[k3], beside).wait_recv()
                send(d_col, k3, low, dxs.at[k3], dxr.at[k3], across).wait_recv()
                core_send(3, k3).start()

        lax.fori_loop(11, 16, visit, 0)
        return carry

    lax.fori_loop(0, lines + 4, step, 0)

    q = lax.broadcasted_iota(jnp.int32, (16, rows), 0)
    plane_base = jnp.where(q < 8, (bo * 2 + q % 2) * block_rows, jnp.where(q < 12, 0, -block_rows)).astype(f32)
    plane_arrow = jnp.where(q_row < 8, q_row // 2, q_row % 4)

    def plane_ranks(k, carry):
        rank_ref[k] = ranks(held[mine, k, pl.ds(rows, 16), pl.ds(0, rows)], plane_arrow, plane_base)[1]
        return carry

    lax.fori_loop(0, lines, plane_ranks, 0)

    def turn(i, carry):
        part = pl.ds(pl.multiple_of(i * 128, 128), 128)
        for kind in range(2):
            place_row[kind, :, part] = place_col[kind, part, :].T[0:8, :]
        return carry

    lax.fori_loop(0, place_row.shape[2] // 128, turn, 0)
    piece = 256
    row_id = lax.broadcasted_iota(jnp.int32, (piece, place_row.shape[2]), 0).astype(f32)

    def unpack(i, carry):
        part = pl.ds(pl.multiple_of(i * piece, piece), piece)
        for kind, out in ((0, x_ref), (1, xh_ref)):
            target = place_row[kind, 0:1, :] - (i * piece).astype(f32)
            select = jnp.where(row_id == target, 1.0, 0.0).astype(bf16)
            out[part, :] = jnp.dot(select, packed[kind], preferred_element_type=f32).astype(bf16)
        return carry

    lax.fori_loop(0, block_rows // piece, unpack, 0)

    def drain(k, carry):
        @pl.when((k <= bo) & (bo < lines - 1))
        def _():
            z_up(k).wait_send()

        @pl.when((k >= bo) & (bo > 0))
        def _():
            z_down(k).wait_send()

        x_send(k).wait_send()
        y_send(k).wait_send()
        dy_send(k).wait_send()
        dx_send(k).wait_send()
        for kind in range(4):
            core_send(kind, k).wait_send()
        return carry

    lax.fori_loop(0, lines, drain, 0)


def gather_blocks(features, positions, nb, cap, block_rows):
    rows, width = features.shape
    n_dev = 4 * nb
    lines = nb // 2
    padded = rows + 16
    slots = n_dev * cap
    dma = pltpu.SemaphoreType.DMA
    vmem = pl.BlockSpec(memory_space=pltpu.VMEM)
    bf16 = jnp.bfloat16
    return pl.pallas_call(
        functools.partial(gather_kernel, (nb, rows, cap, block_rows)),
        out_shape=(
            jax.ShapeDtypeStruct((block_rows, width), bf16),
            jax.ShapeDtypeStruct((block_rows, width), bf16),
            jax.ShapeDtypeStruct((slots, block_rows), bf16),
            jax.ShapeDtypeStruct((slots, block_rows), bf16),
            jax.ShapeDtypeStruct((lines, 16, rows), jnp.float32),
        ),
        in_specs=[vmem, vmem],
        out_specs=(vmem,) * 5,
        scratch_shapes=[
            pltpu.VMEM((8, lines, padded, width), bf16),
            pltpu.VMEM((16, width), jnp.float32),
            pltpu.VMEM((2, slots, width), bf16),
            pltpu.VMEM((2, slots, 128), jnp.float32),
            pltpu.VMEM((2, 8, slots), jnp.float32),
            dma((2, lines)), dma((lines,)),
            dma((lines,)), dma((lines,)), dma((lines,)), dma((lines,)),
            dma((lines,)), dma((lines,)), dma((lines,)), dma((lines,)),
            dma((4, lines)), dma((4, lines)), dma(()),
        ],
        compiler_params=pltpu.CompilerParams(
            collective_id=0, has_side_effects=True, vmem_limit_bytes=60 * 2**20),
        name="gather_blocks",
    )(features, positions)


def return_kernel(dims, x_ref, xh_ref, st_ref, sth_ref, rank_ref, tiles_ref, features_ref, diag_hbm,
                  column_hbm, row_hbm, up_hbm, down_hbm, out_ref, blocks, up_weight, down_weight, early,
                  acc, masks, arm, results, outgoing, incoming, partial, column_in, load_sem, psend, precv, zsend, zrecv):
    nb, cap = dims
    lines = nb // 2
    block_rows, width = x_ref.shape
    a, b = lax.axis_index("arrow"), lax.axis_index("blk")
    bo, bi = b // 2, b % 2
    me = bi * 4 + a
    f32, bf16 = jnp.float32, jnp.bfloat16
    edge = tiles_ref.shape[1]
    tile = block_rows // edge

    loads = [pltpu.make_async_copy(ref, blocks.at[i], load_sem.at[i])
             for i, ref in enumerate((diag_hbm, column_hbm, row_hbm))]
    loads.append(pltpu.make_async_copy(up_hbm, up_weight, load_sem.at[3]))
    loads.append(pltpu.make_async_copy(down_hbm, down_weight, load_sem.at[4]))
    for load in loads:
        load.start()

    barrier = pltpu.get_barrier_semaphore()

    def greet(to, carry):
        @pl.when(to != me)
        def _():
            pl.semaphore_signal(barrier, inc=1, device_id=(to % 4, bo * 2 + to // 4),
                                device_id_type=MESH)
        return carry

    def greet_column(k, carry):
        @pl.when(k != bo)
        def _():
            pl.semaphore_signal(barrier, inc=1, device_id=(a, k * 2 + bi), device_id_type=MESH)
        return carry

    lax.fori_loop(0, 8, greet, 0)
    lax.fori_loop(0, lines, greet_column, 0)
    spread = (lax.broadcasted_iota(jnp.int32, (edge, block_rows), 1) // tile
              == lax.broadcasted_iota(jnp.int32, (edge, block_rows), 0)).astype(f32)
    for kind in range(3):
        masks[kind] = jnp.dot(tiles_ref[kind].astype(f32), spread, preferred_element_type=f32)

    def masked(kind, i):
        rows = pl.ds(pl.multiple_of(i * tile, tile), tile)
        return blocks[kind, rows, :] * masks[kind, pl.ds(i, 1), :].astype(bf16)

    for load in loads[:3]:
        load.wait()

    def block_tile(i, carry):
        rows = pl.ds(pl.multiple_of(i * tile, tile), tile)
        arm[rows, :] = jnp.dot(masked(2, i), x_ref[...], preferred_element_type=f32).astype(bf16)
        results[rows, :] = (
            jnp.dot(masked(0, i), x_ref[...], preferred_element_type=f32)
            + jnp.dot(masked(1, i), xh_ref[...], preferred_element_type=f32)).astype(bf16)
        return carry

    lax.fori_loop(0, edge, block_tile, 0)
    pl.semaphore_wait(barrier, 7 + lines - 1)

    def plane_copy(k, to, frm):
        return pltpu.make_async_remote_copy(
            src_ref=outgoing.at[k, to], dst_ref=incoming.at[k, frm], send_sem=psend.at[k, to],
            recv_sem=precv.at[k, frm], device_id=(to % 4, bo * 2 + to // 4), device_id_type=MESH)

    def column_copy(to, frm):
        return pltpu.make_async_remote_copy(
            src_ref=partial.at[to], dst_ref=column_in.at[frm], send_sem=zsend.at[to],
            recv_sem=zrecv.at[frm], device_id=(a, to * 2 + bi), device_id_type=MESH)

    def far_first(body):
        def step(i, carry):
            late = lines - 1 - i // 2
            k = bo + (i % 2 * 2 - 1) * late
            pl.when((k >= 0) & (k < lines) & ((late > 0) | (i % 2 == 0)))(functools.partial(body, k))
            return carry
        lax.fori_loop(0, 2 * lines, step, 0)

    def send_chunk(k):
        chunk = 8 * cap
        rows = pl.ds(pl.multiple_of(k * chunk, 16), chunk)
        for kind, select, values in ((0, st_ref, results), (1, sth_ref, arm)):
            found = jnp.dot(select[rows, :], values[...], preferred_element_type=f32).astype(bf16)
            outgoing[k, :, pl.ds(kind * cap, cap), :] = found.reshape(8, cap, width)

        def one(to, carry):
            @pl.when(to != me)
            def _():
                plane_copy(k, to, me).start()
            return carry

        lax.fori_loop(0, 8, one, 0)
        incoming[k, me] = outgoing[k, me]

    far_first(send_chunk)
    loads[3].wait()
    hidden_width = up_weight.shape[1]
    part = 512

    def first_half(i, carry):
        lanes = pl.ds(pl.multiple_of(i * part, part), part)
        early[:, lanes] = jnp.dot(features_ref[...], up_weight[pl.ds(0, width), lanes],
                                  preferred_element_type=f32)
        return carry

    lax.fori_loop(0, hidden_width // part, first_half, 0)
    loads[4].wait()
    lane = lax.broadcasted_iota(jnp.int32, (16, 16 * cap), 1)
    frm = lane // (2 * cap)
    source = jnp.where(lane // cap % 2 == 0, frm % 4 * 2 + frm // 4, 8 + frm % 4)
    expand = (lax.broadcasted_iota(jnp.int32, (16, 16 * cap), 0) == source).astype(f32).astype(bf16)
    slot = (lax.broadcasted_iota(jnp.int32, (1, 16 * cap), 1) % cap).astype(f32)

    def sum_chunk(k):
        held = lax.dot_general(rank_ref[k].astype(bf16), expand, (((0,), (0,)), ((), ())),
                               preferred_element_type=f32)
        gather = jnp.where(held == slot, 1.0, 0.0).astype(bf16)

        def one(frm, carry):
            @pl.when(frm != me)
            def _():
                plane_copy(k, me, frm).wait_recv()
            return carry

        lax.fori_loop(0, 8, one, 0)
        partial[k] = jnp.dot(gather, incoming[k].reshape(16 * cap, width),
                             preferred_element_type=f32).astype(bf16)

        @pl.when(k != bo)
        def _():
            column_copy(k, bo).start()

    far_first(sum_chunk)

    def drain(k, carry):
        def one(to, inner):
            @pl.when(to != me)
            def _():
                plane_copy(k, to, me).wait_send()
            return inner

        lax.fori_loop(0, 8, one, 0)

        @pl.when(k != bo)
        def _():
            column_copy(k, bo).wait_send()
            column_copy(bo, k).wait_recv()
        return carry

    lax.fori_loop(0, lines, drain, 0)
    column_in[bo] = partial[bo]
    aggregate = jnp.sum(column_in[...].astype(f32), axis=0).astype(bf16)
    partial[0] = aggregate
    acc[...] = jnp.zeros(acc.shape, f32)

    def mlp(i, carry):
        lanes = pl.ds(pl.multiple_of(i * part, part), part)
        value = early[:, lanes] + jnp.dot(partial[0], up_weight[pl.ds(width, width), lanes],
                                          preferred_element_type=f32)
        hidden = (value / (1.0 + jnp.exp(-value))).astype(bf16)
        acc[...] += jnp.dot(hidden, down_weight[lanes, :], preferred_element_type=f32)
        return carry

    lax.fori_loop(0, hidden_width // part, mlp, 0)
    out_ref[...] = acc[...].astype(bf16)


def return_rows(x, xh, select, select_head, plane_rank, tiles, features, diag, column, row, up, down,
                nb, cap):
    block_rows, width = x.shape
    lines, _, rows = plane_rank.shape
    dma = pltpu.SemaphoreType.DMA
    vmem = pl.BlockSpec(memory_space=pltpu.VMEM)
    hbm = pl.BlockSpec(memory_space=pl.ANY)
    bf16 = jnp.bfloat16
    return pl.pallas_call(
        functools.partial(return_kernel, (nb, cap)),
        out_shape=jax.ShapeDtypeStruct((rows, width), bf16),
        in_specs=[vmem] * 7 + [hbm] * 5,
        out_specs=vmem,
        scratch_shapes=[
            pltpu.VMEM((3, block_rows, block_rows), bf16),
            pltpu.VMEM(up.shape, bf16),
            pltpu.VMEM(down.shape, bf16),
            pltpu.VMEM((rows, up.shape[1]), jnp.float32),
            pltpu.VMEM((rows, width), jnp.float32),
            pltpu.VMEM((3, tiles.shape[1], block_rows), jnp.float32),
            pltpu.VMEM((block_rows, width), bf16),
            pltpu.VMEM((block_rows, width), bf16),
            pltpu.VMEM((lines, 8, 2 * cap, width), bf16),
            pltpu.VMEM((lines, 8, 2 * cap, width), bf16),
            pltpu.VMEM((lines, rows, width), bf16),
            pltpu.VMEM((lines, rows, width), bf16),
            dma((5,)), dma((lines, 8)), dma((lines, 8)), dma((lines,)), dma((lines,)),
        ],
        compiler_params=pltpu.CompilerParams(
            collective_id=1, has_side_effects=True, vmem_limit_bytes=60 * 2**20),
        name="return_rows",
    )(x, xh, select, select_head, plane_rank, tiles, features, diag, column, row, up, down)


def body(
    features, positions, diag_values, column_values, row_values, tile_masks, up_weight, down_weight
):
    rows = features.shape[0]
    nb = lax.axis_size("blk")
    block_rows = diag_values.shape[0]
    capacity = rows // nb + max(rows // (2 * nb), 1)
    cap = (capacity + 15) // 16 * 16
    x, x_head, select, select_head, plane_rank = gather_blocks(
        features, positions, nb, cap, block_rows)
    return return_rows(x, x_head, select, select_head, plane_rank, tile_masks, features,
                       diag_values, column_values, row_values, up_weight, down_weight, nb, cap)


def solution(mesh):
    in_specs = (
        P(("arrow", "blk"), None),
        P(None, ("arrow", "blk")),
        P("arrow", "blk"),
        P("arrow", "blk"),
        P("arrow", "blk"),
        P(None, "arrow", "blk"),
        P(),
        P(),
    )
    out_specs = P(("arrow", "blk"), None)
    return jax.shard_map(body, mesh=mesh, in_specs=in_specs, out_specs=out_specs, check_vma=False)
```
